32 devices in a mesh: groups: 2 (over y), ctx: 4 (over z), dp: 4 (over x, core).
Axes of the slice: x: 2, y: 2, z: 4, core: 2. Of those that a mesh axis runs over, the one named last changes fastest.
Arguments:
- inputs: bfloat16 [8, 1536, 1024], P(('groups', 'dp'), 'ctx'), parts along dimension 0, may hold values from -6 to 6
- queries: bfloat16 [8, 1536, 1024], P(('groups', 'dp'), 'ctx'), parts along dimension 0, may hold values from -96 to 96
- cotangent: bfloat16 [8, 1536, 1024], P(('groups', 'dp'), 'ctx'), parts along dimension 0, may hold values from -6 to 6
- length_proj: bfloat16 [1536, 2, 256], P('ctx'), may hold values from -0.15625 to 0.15625
- key_value_weight: bfloat16 [1024, 2, 1024], P(None, None, 'ctx'), may hold values from -0.1875 to 0.1875
Outputs:
- query_grad: bfloat16 [8, 1536, 1024], P(('groups', 'dp'), 'ctx'), parts along dimension 0
- input_grad: bfloat16 [8, 1536, 1024], P(('groups', 'dp'), 'ctx'), parts along dimension 0
- length_grad: float32 [3072, 2, 256], P(('groups', 'ctx', 'dp')), parts along dimension 0
- weight_grad: float32 [2048, 2, 1024], P(('groups', 'dp'), None, 'ctx'), parts along dimension 0
The draws below stay inside these ranges and needn't reach their ends.
There are 2 independent parts, one for each index of `groups`. The reference program is written for one: setup_inputs(seed, part) draws one part's arguments, and reference() takes and returns one part's arrays. A program takes and returns all parts, laid end to end along the dimension named above; an argument that names none is the same for every part. Nothing has to cross between parts.
All inputs are finite; a program needn't handle non-finite values.
Results may differ from the reference program's by a relative error of at most 0.018.
The reference program's roundings to bfloat16 on the way count: a program that leaves them out, or rounds other values in their place, can miss the bound.
Values may be sent and summed in bfloat16 or wider, within the bound.
No kernel may reach another device: no remote copies, remote signals or barrier semaphores. Data moves between devices by JAX's collectives and lax.ppermute only.
A program may use at most 64 MiB of HBM per device.

```python
import jax
import jax.numpy as jnp
from jax import lax

D = 1024
HEADS = 16
DH = 64
KP = 256
LENGTH = 1536
BATCH = 4


def draw_queries(key, part):
    key = jax.random.fold_in(key, 11)
    base = jnp.clip(jax.random.normal(key, (BATCH, LENGTH, D), jnp.float32), -4.0, 4.0)
    return base.astype(jnp.bfloat16)


def block_scale(rng, extent, pieces, least, largest):
    def one(position, parts):
        draws = jax.random.uniform(jax.random.fold_in(jax.random.fold_in(rng, 6), position), (parts,), jnp.float32, least / len(pieces), largest / len(pieces))
        return jnp.repeat(jnp.exp(draws), extent[position] // parts).reshape((-1,) + (1,) * (len(extent) - position - 1))

    gain = one(*pieces[0])
    for cut in pieces[1:]:
        gain = gain * one(*cut)
    return gain


def centred(own_key, dims, scale, reach, shards=(), dtype=jnp.bfloat16):
    entries = scale * jax.random.normal(own_key, dims, jnp.float32)
    if shards:
        entries = entries * block_scale(own_key, dims, shards, -0.22, 0.18)
    return jnp.clip(entries, -reach, reach).astype(dtype)


def setup_inputs(seed: int = 0, part: int = 0) -> dict:
    key_of = jax.random.split(jax.random.key(seed), 6)
    own_keys = jax.random.split(jax.random.fold_in(key_of[5], part), 6)
    inputs = centred(own_keys[0], (BATCH, LENGTH, D), 1.0, 6.0, ((0, 4), (1, 4)))
    queries = draw_queries(jax.random.fold_in(jax.random.fold_in(key_of[5], part), 71), part)
    cotangent = centred(own_keys[2], (BATCH, LENGTH, D), 1.0, 6.0, ((0, 4), (1, 4)))
    length_proj = centred(key_of[3], (LENGTH, 2, KP), LENGTH ** -0.5, 0.15625, ((0, 4),))
    key_value_weight = centred(key_of[4], (D, 2, D), D ** -0.5, 0.1875, ((2, 4),))
    return dict(inputs=inputs, queries=queries, cotangent=cotangent, length_proj=length_proj, key_value_weight=key_value_weight)


def one_sequence(tokens, query_row_block, grad_rows, length_proj, key_value_weight):
    scale = DH ** -0.5
    length_compressed = jnp.einsum("lsk,ld->skd", length_proj.astype(jnp.float32), tokens.astype(jnp.float32)).astype(jnp.bfloat16)
    length_projected = jnp.einsum("fpg,gfv->fpv", length_compressed.astype(jnp.float32), key_value_weight.astype(jnp.float32)).astype(jnp.bfloat16)
    keys = length_projected[0].reshape(KP, HEADS, DH).astype(jnp.float32)
    values = length_projected[1].reshape(KP, HEADS, DH).astype(jnp.float32)
    query_heads = query_row_block.reshape(-1, HEADS, DH).astype(jnp.float32)
    grad_heads = grad_rows.reshape(-1, HEADS, DH).astype(jnp.float32)
    scores = jnp.einsum("lhd,khd->hlk", query_heads, keys) * scale
    probs = jax.nn.softmax(scores, axis=-1)
    probs_low = probs.astype(jnp.bfloat16).astype(jnp.float32)
    dprobs = jnp.einsum("lhd,khd->hlk", grad_heads, values)
    delta = jnp.sum(probs * dprobs, axis=-1, keepdims=True)
    dscores = (probs * (dprobs - delta) * scale).astype(jnp.bfloat16).astype(jnp.float32)
    query_grad = jnp.einsum("hlk,khd->lhd", dscores, keys).astype(jnp.bfloat16).reshape(-1, D)
    key_part = jnp.einsum("hlk,lhd->khd", dscores, query_heads).reshape(KP, D)
    value_part = jnp.einsum("hlk,lhd->khd", probs_low, grad_heads).reshape(KP, D)
    projection_gradient = jnp.stack([key_part, value_part]).astype(jnp.bfloat16).astype(jnp.float32)
    compression_gradient = jnp.einsum("jwt,ljt->jwl", projection_gradient, key_value_weight.astype(jnp.float32)).astype(jnp.bfloat16).astype(jnp.float32)
    input_grad = jnp.einsum("lsk,skd->ld", length_proj.astype(jnp.float32), compression_gradient).astype(jnp.bfloat16)
    length_term = jnp.einsum("ld,skd->lsk", tokens.astype(jnp.float32), compression_gradient)
    weight_contribution = jnp.einsum("fib,fin->bfn", length_compressed.astype(jnp.float32), projection_gradient)
    return query_grad, input_grad, length_term, weight_contribution


def reference(inputs, queries, cotangent, length_proj, key_value_weight):
    def step(carry, items):
        tokens, query_row_block, grad_rows = items
        query_grad, input_grad, length_term, weight_contribution = one_sequence(tokens, query_row_block, grad_rows, length_proj, key_value_weight)
        return (carry[0] + length_term, carry[1] + weight_contribution), (query_grad, input_grad)

    start = (jnp.zeros(length_proj.shape, jnp.float32), jnp.zeros(key_value_weight.shape, jnp.float32))
    totals, outputs = lax.scan(step, start, (inputs, queries, cotangent))
    return outputs[0], outputs[1], totals[0], totals[1]
```

```python
import functools

import jax
import jax.numpy as jnp
from jax import lax
from jax.experimental import pallas as pl
from jax.experimental.pallas import tpu as pltpu
from jax.sharding import PartitionSpec as P

HEADS = 16
DH = 64
KP = 256
BF = jnp.bfloat16
F32 = jnp.float32
VMEM_LIMIT = 40 * 1024 * 1024


def dot(a, b, ca, cb):
    return lax.dot_general(a, b, (((ca,), (cb,)), ((), ())), preferred_element_type=F32)


def call(body, outs, args, scratch=(), flops=0, name=None):
    nbytes = sum(a.size * a.dtype.itemsize for a in args) + sum(o.size * o.dtype.itemsize for o in outs)
    vmem = pl.BlockSpec(memory_space=pltpu.VMEM)
    return pl.pallas_call(
        body,
        out_shape=outs,
        in_specs=[pl.BlockSpec(memory_space=pltpu.SMEM)] + [vmem] * (len(args) - 1),
        out_specs=[vmem] * len(outs),
        scratch_shapes=list(scratch),
        compiler_params=pltpu.CompilerParams(vmem_limit_bytes=VMEM_LIMIT),
        cost_estimate=pl.CostEstimate(flops=flops, bytes_accessed=nbytes, transcendentals=0),
        name=name,
    )(*args)


def shape(dims, dtype):
    return jax.ShapeDtypeStruct(dims, dtype)


def compress_body(n, plane, rows, idx, e_own, e_core, *rest):
    blocks, out, e_all = rest[:n], rest[n], rest[n + 1]
    part = rows // plane
    for c, e in enumerate((e_own, e_core)):
        for a in range(plane // 2):
            piece = idx[2 + a] ^ c
            for k in range(n):
                row = pl.multiple_of(k * rows + piece * part, 16)
                e_all[pl.ds(row, part), :] = e[a, k]
    total = dot(e_all[0:rows, :], blocks[0][...], 0, 0)
    for k in range(1, n):
        total += dot(e_all[k * rows : (k + 1) * rows, :], blocks[k][...], 0, 0)
    out[...] = total.astype(BF)


def project_body(n, own, idx, *rest):
    parts, w, keys, values = rest[:n], rest[n], rest[n + 1], rest[n + 2]
    for s, out in enumerate((keys, values)):
        total = None
        for k in range(n):
            row = pl.multiple_of(lax.rem(idx[0] - k + n, n) * own, own)
            term = dot(parts[k][s * KP : (s + 1) * KP, :], w[pl.ds(row, own), s * own : (s + 1) * own], 1, 0)
            total = term if total is None else total + term
        out[...] = total.astype(BF)


def attention_body(heads, first, last, idx, keys, values, qg, *rest):
    if first:
        query_grad, acc = rest
    else:
        before, query_grad, acc = rest
    q, g, kk, vv = qg[0], qg[1], keys[...], values[...]
    scale = DH**-0.5
    lane = lax.broadcasted_iota(jnp.int32, kk.shape, 1)
    grad_q = key_part = value_part = None
    for h in range(heads):
        mask = (lane >= h * DH) & (lane < (h + 1) * DH)
        k_h = jnp.where(mask, kk, jnp.zeros_like(kk))
        v_h = jnp.where(mask, vv, jnp.zeros_like(vv))
        scores = dot(k_h, q, 1, 1)
        e = jnp.exp((scores - jnp.max(scores, axis=0, keepdims=True)) * scale)
        p = e * (1.0 / jnp.sum(e, axis=0, keepdims=True))
        dp = dot(v_h, g, 1, 1)
        delta = jnp.sum(p * dp, axis=0, keepdims=True)
        ds = (p * (dp - delta) * scale).astype(BF)
        term_q = dot(ds, k_h, 0, 0)
        term_k = jnp.where(mask, dot(ds, q, 1, 0), 0.0)
        term_v = jnp.where(mask, dot(p.astype(BF), g, 1, 0), 0.0)
        grad_q = term_q if h == 0 else grad_q + term_q
        key_part = term_k if h == 0 else key_part + term_k
        value_part = term_v if h == 0 else value_part + term_v
    query_grad[...] = grad_q.astype(BF)
    if not first:
        key_part = key_part + before[0]
        value_part = value_part + before[1]
    acc[0] = key_part.astype(acc.dtype)
    acc[1] = value_part.astype(acc.dtype)


def weight_body(n, own, idx, *rest):
    parts, grad, out = rest[:n], rest[n], rest[n + 1]
    for k in range(n):
        row = pl.multiple_of(lax.rem(idx[0] - k + n, n) * own, own)
        for s in range(2):
            out[pl.ds(row, own), s * own : (s + 1) * own] = dot(parts[k][s * KP : (s + 1) * KP, :], grad[s], 0, 0)


def tail_body(n, nd, own, idx, *rest):
    grads, w, e, x, input_grad, length_terms, cg = rest[:n], *rest[n:]
    width = n * own
    for s in range(2):
        total = None
        for k in range(n):
            row = pl.multiple_of(lax.rem(idx[0] - k + n, n) * width, width)
            term = dot(grads[k][s], w[pl.ds(row, width), s * own : (s + 1) * own], 1, 1)
            total = term if total is None else total + term
        cg[s * KP : (s + 1) * KP, :] = total.astype(BF)
    both = cg[...]
    part = x.shape[0] // nd
    for a in range(nd):
        row = pl.multiple_of((idx[1] ^ a) * part, 16)
        length_terms[a] = dot(x[pl.ds(row, part), :], both, 1, 1)
    input_grad[...] = dot(e[...], both, 1, 0).astype(BF)


def place_body(n, own, idx, *rest):
    out = rest[n]
    for k in range(n):
        col = pl.multiple_of(lax.rem(idx[0] + k, n) * own, own)
        out[:, pl.ds(col, own)] = rest[k][...]


def by_heads(ng, n, nd, inputs, queries, cotangent, length_proj, key_value_weight):
    tokens, query_rows, grad_rows = inputs[0], queries[0], cotangent[0]
    rows, width = tokens.shape
    own = width // n
    plane = ng * nd
    g, i, d = lax.axis_index("groups"), lax.axis_index("ctx"), lax.axis_index("dp")
    m = g * nd + d
    flips = [(gy, dx) for gy in range(2) for dx in range(2)]
    idx = jnp.stack([i, d] + [(g ^ gy) * nd + (d ^ (2 * dx)) for gy, dx in flips]).astype(jnp.int32)

    def rot(k):
        return [(j, (j + k) % n) for j in range(n)]

    def swap(a):
        return [(j, j ^ a) for j in range(nd)]

    def chunk(x, k):
        return lax.dynamic_slice_in_dim(x, lax.rem(i + k, n) * own, own, 1)

    def gather(x):
        return [x] + [lax.ppermute(x, "ctx", rot(k)) for k in range(1, n)]

    part = rows // plane
    piece = lax.dynamic_slice_in_dim(length_proj, m * part, part, 0).reshape(part, 2 * KP)
    line = jnp.stack(gather(piece))
    across = [line]
    for gy, dx in flips[1:]:
        perm = [
            (a * nd + b, (a ^ gy) * nd + (b ^ (2 * dx))) for a in range(ng) for b in range(nd)
        ]
        across.append(lax.ppermute(line, ("groups", "dp"), perm))
    e_own = jnp.stack(across)
    e_core = lax.ppermute(e_own, "dp", swap(1))

    blocks = [chunk(tokens, 0)]
    blocks += [lax.ppermute(chunk(tokens, k), "ctx", rot(k)) for k in range(1, n)]
    compressed = call(
        functools.partial(compress_body, n, plane, rows),
        [shape((2 * KP, own), BF)],
        [idx, e_own, e_core, *blocks],
        [pltpu.VMEM((n * rows, 2 * KP), BF)],
        flops=4 * KP * own * n * rows,
        name="compress",
    )[0]
    parts = gather(compressed)

    w = key_value_weight.reshape(width, 2 * own)
    w_piece = lax.dynamic_slice_in_dim(w, m * (width // plane), width // plane, 0)
    w_all = lax.all_gather(w_piece, ("ctx", "groups", "dp"), axis=0, tiled=True)

    qg = [jnp.stack([chunk(query_rows, k), chunk(grad_rows, k)]) for k in range(n)]
    qg = [qg[0]] + [lax.ppermute(qg[k], "ctx", rot(k)) for k in range(1, n)]

    keys, values = call(
        functools.partial(project_body, n, own),
        [shape((KP, own), BF)] * 2,
        [idx, *parts, w],
        flops=4 * KP * width * own,
        name="project",
    )
    heads = own // DH
    query_grads, acc = [], None
    for k in range(n):
        args = [idx, keys, values, qg[k]] + ([] if k == 0 else [acc])
        grad, acc = call(
            functools.partial(attention_body, heads, k == 0, k == n - 1),
            [shape((rows, own), BF), shape((2, KP, own), BF if k == n - 1 else F32)],
            args,
            flops=10 * heads * rows * KP * own,
            name="attention",
        )
        query_grads.append(grad)
    grads = gather(acc)

    weight = call(
        functools.partial(weight_body, n, own),
        [shape((width, 2 * own), F32)],
        [idx, *parts, acc],
        flops=4 * KP * own * width,
        name="weight",
    )[0]
    weight_grad = lax.psum_scatter(weight, "dp", scatter_dimension=0, tiled=True)
    weight_grad = weight_grad.reshape(-1, 2, own)

    returned = [query_grads[0]]
    returned += [lax.ppermute(query_grads[k], "ctx", rot(n - k)) for k in range(1, n)]

    input_grad, terms = call(
        functools.partial(tail_body, n, nd, own),
        [shape((rows, width), BF), shape((nd, rows // nd, 2 * KP), F32)],
        [idx, *grads, w_all, length_proj.reshape(rows, 2 * KP), tokens],
        [pltpu.VMEM((2 * KP, width), BF)],
        flops=4 * KP * width * width + 8 * KP * rows * width,
        name="tail",
    )
    length_grad = terms[0]
    for a in range(1, nd):
        length_grad = length_grad + lax.ppermute(terms[a], "dp", swap(a))
    length_grad = length_grad.reshape(-1, 2, KP)

    query_grad = call(
        functools.partial(place_body, n, own),
        [shape((rows, width), BF)],
        [idx, *returned],
        name="place",
    )[0]
    return query_grad[None], input_grad[None], length_grad, weight_grad


def by_positions(inputs, queries, cotangent, length_proj, key_value_weight):
    scale = DH ** (-0.5)
    tokens = inputs[0]
    query_row_block = queries[0]
    grad_rows = cotangent[0]
    rows = tokens.shape[0]
    full_width = key_value_weight.shape[0]
    compress = jnp.einsum("lsk,ld->skd", length_proj, tokens, preferred_element_type=jnp.float32)
    length_compressed = lax.psum(compress, "ctx").astype(jnp.bfloat16)
    own_proj = jnp.einsum(
        "skd,dsc->skc", length_compressed, key_value_weight, preferred_element_type=jnp.float32
    ).astype(jnp.bfloat16)
    length_projected = lax.all_gather(own_proj, "ctx", axis=2, tiled=True)
    keys = length_projected[0].reshape(KP, HEADS, DH)
    values = length_projected[1].reshape(KP, HEADS, DH)
    query_heads = query_row_block.reshape(rows, HEADS, DH)
    grad_heads = grad_rows.reshape(rows, HEADS, DH)
    scores = (
        jnp.einsum("lhd,khd->hlk", query_heads, keys, preferred_element_type=jnp.float32) * scale
    )
    probs = jax.nn.softmax(scores, axis=-1)
    probs_low = probs.astype(jnp.bfloat16)
    dprobs = jnp.einsum("lhd,khd->hlk", grad_heads, values, preferred_element_type=jnp.float32)
    delta = jnp.sum(probs * dprobs, axis=-1, keepdims=True)
    dscores = (probs * (dprobs - delta) * scale).astype(jnp.bfloat16)
    query_grad = jnp.einsum(
        "hlk,khd->lhd", dscores, keys, preferred_element_type=jnp.float32
    ).astype(jnp.bfloat16)
    query_grad = query_grad.reshape(1, rows, full_width)
    key_part = jnp.einsum("hlk,lhd->khd", dscores, query_heads, preferred_element_type=jnp.float32)
    value_part = jnp.einsum(
        "hlk,lhd->khd", probs_low, grad_heads, preferred_element_type=jnp.float32
    )
    partial_grad = jnp.stack([key_part.reshape(KP, full_width), value_part.reshape(KP, full_width)])
    own_grad = lax.psum_scatter(partial_grad, "ctx", scatter_dimension=2, tiled=True).astype(
        jnp.bfloat16
    )
    grad_term = jnp.einsum(
        "skc,dsc->skd", own_grad, key_value_weight, preferred_element_type=jnp.float32
    )
    compression_gradient = lax.psum(grad_term, "ctx").astype(jnp.bfloat16)
    input_grad = jnp.einsum(
        "lsk,skd->ld", length_proj, compression_gradient, preferred_element_type=jnp.float32
    ).astype(jnp.bfloat16)
    input_grad = input_grad.reshape(1, rows, full_width)
    length_grad = lax.psum_scatter(
        jnp.einsum("ld,skd->lsk", tokens, compression_gradient, preferred_element_type=jnp.float32),
        "dp",
        scatter_dimension=0,
        tiled=True,
    )
    weight_grad = lax.psum_scatter(
        jnp.einsum("skd,skc->dsc", length_compressed, own_grad, preferred_element_type=jnp.float32),
        "dp",
        scatter_dimension=0,
        tiled=True,
    )
    return (query_grad, input_grad, length_grad, weight_grad)


def solution(mesh):
    ng, n, nd = (mesh.shape[a] for a in ("groups", "ctx", "dp"))

    def local(*args):
        rows, width = args[0].shape[1:]
        fits = ng == 2 and nd == 4 and width % (n * 128) == 0 and HEADS % n == 0 and rows % 128 == 0
        if fits:
            return by_heads(ng, n, nd, *args)
        return by_positions(*args)

    in_specs = (
        P(("groups", "dp"), "ctx", None),
        P(("groups", "dp"), "ctx", None),
        P(("groups", "dp"), "ctx", None),
        P("ctx", None, None),
        P(None, None, "ctx"),
    )
    out_specs = (
        P(("groups", "dp"), "ctx", None),
        P(("groups", "dp"), "ctx", None),
        P(("groups", "ctx", "dp"), None, None),
        P(("groups", "dp"), None, "ctx"),
    )
    return jax.shard_map(local, mesh=mesh, in_specs=in_specs, out_specs=out_specs, check_vma=False)
```

```python
import functools

import jax
import jax.numpy as jnp
from jax import lax
from jax.experimental import pallas as pl
from jax.experimental.pallas import tpu as pltpu
from jax.sharding import PartitionSpec as P

HEADS = 16
DH = 64
KP = 256
BF = jnp.bfloat16
F32 = jnp.float32
VMEM_LIMIT = 24 * 1024 * 1024


def dot(a, b, ca, cb):
    return lax.dot_general(a, b, (((ca,), (cb,)), ((), ())), preferred_element_type=F32)


def call(body, outs, args, after=(), scratch=(), name=None):
    vmem = pl.BlockSpec(memory_space=pltpu.VMEM)

    def run(*refs):
        body(*refs[: len(args)], *refs[len(args) + len(after) :])

    return pl.pallas_call(
        run,
        out_shape=outs,
        in_specs=[pl.BlockSpec(memory_space=pltpu.SMEM)]
        + [vmem] * (len(args) - 1)
        + [pl.BlockSpec(memory_space=pl.ANY)] * len(after),
        out_specs=[vmem] * len(outs),
        scratch_shapes=list(scratch),
        compiler_params=pltpu.CompilerParams(vmem_limit_bytes=VMEM_LIMIT),
        cost_estimate=pl.CostEstimate(flops=1, bytes_accessed=1, transcendentals=0),
        name=name,
    )(*args, *after)


def gate(arrays, after, name):
    return pl.pallas_call(
        lambda *refs: None,
        out_shape=[shape(a.shape, a.dtype) for a in arrays],
        in_specs=[pl.BlockSpec(memory_space=pl.ANY)] * (len(arrays) + len(after)),
        out_specs=[pl.BlockSpec(memory_space=pl.ANY)] * len(arrays),
        input_output_aliases={k: k for k in range(len(arrays))},
        cost_estimate=pl.CostEstimate(flops=1, bytes_accessed=1, transcendentals=0),
        name=name,
    )(*arrays, *after)


def shape(dims, dtype):
    return jax.ShapeDtypeStruct(dims, dtype)


def pack_body(n, own, idx, *rest):
    x, outs = rest[0], rest[1:]
    for k in range(n):
        col = pl.multiple_of((idx[0] ^ k) * own, own)
        outs[k][...] = x[:, pl.ds(col, own)]


def pack_pair_body(own, k, idx, q, g, out):
    col = pl.multiple_of((idx[0] ^ k) * own, own)
    out[0] = q[:, pl.ds(col, own)]
    out[1] = g[:, pl.ds(col, own)]


def join_ends_body(idx, mine, side, near, far, out):
    inner = (idx[0] == 1) | (idx[0] == 2)
    out[0] = mine[...]
    out[1] = side[...]
    for a in range(2):
        out[2 + a] = pick(inner, near[1 - a], far[a])


def join_body(idx, *rest):
    out = rest[-1]
    for k, x in enumerate(rest[:-1]):
        out[k] = x[...]


def slice_body(idx, x, out):
    rows = out.shape[0]
    out[...] = x[pl.ds(pl.multiple_of(idx[2] * rows, rows), rows), :]


def compress_body(n, plane, rows, idx, e_own, e_core, *rest):
    blocks, out, e_all = rest[:n], rest[n], rest[n + 1]
    part = rows // plane
    for c, e in enumerate((e_own, e_core)):
        for a in range(plane // 2):
            piece = idx[2 + a] ^ c
            for k in range(n):
                row = pl.multiple_of(k * rows + piece * part, 16)
                e_all[pl.ds(row, part), :] = e[a, k]
    total = dot(e_all[0:rows, :], blocks[0][...], 0, 0)
    for k in range(1, n):
        total += dot(e_all[k * rows : (k + 1) * rows, :], blocks[k][...], 0, 0)
    out[...] = total.astype(BF)


def pick(inner, near, far):
    return jnp.where(inner, near, far)


def project_body(own, idx, mine, side, near, far, w, keys, values, whole):
    inner = (idx[0] == 1) | (idx[0] == 2)
    whole[0] = mine[...]
    whole[1] = side[...]
    for a in range(2):
        whole[2 + a] = pick(inner, near[1 - a], far[a])
    for s, out in enumerate((keys, values)):
        total = None
        for k in range(4):
            row = pl.multiple_of((idx[0] ^ k) * own, own)
            term = dot(whole[k, s * KP : (s + 1) * KP, :], w[pl.ds(row, own), s * own : (s + 1) * own], 1, 0)
            total = term if total is None else total + term
        out[...] = total.astype(BF)


def attention_body(heads, first, last, idx, keys, values, qg, *rest):
    if first:
        query_grad, acc = rest
    else:
        before, query_grad, acc = rest
    q, g, kk, vv = qg[0], qg[1], keys[...], values[...]
    scale = DH**-0.5
    lane = lax.broadcasted_iota(jnp.int32, kk.shape, 1)
    grad_q = key_part = value_part = None
    for h in range(heads):
        mask = (lane >= h * DH) & (lane < (h + 1) * DH)
        k_h = jnp.where(mask, kk, jnp.zeros_like(kk))
        v_h = jnp.where(mask, vv, jnp.zeros_like(vv))
        scores = dot(k_h, q, 1, 1)
        e = jnp.exp((scores - jnp.max(scores, axis=0, keepdims=True)) * scale)
        p = e * (1.0 / jnp.sum(e, axis=0, keepdims=True))
        dp = dot(v_h, g, 1, 1)
        delta = jnp.sum(p * dp, axis=0, keepdims=True)
        ds = (p * (dp - delta) * scale).astype(BF)
        term_q = dot(ds, k_h, 0, 0)
        term_k = jnp.where(mask, dot(ds, q, 1, 0), 0.0)
        term_v = jnp.where(mask, dot(p.astype(BF), g, 1, 0), 0.0)
        grad_q = term_q if h == 0 else grad_q + term_q
        key_part = term_k if h == 0 else key_part + term_k
        value_part = term_v if h == 0 else value_part + term_v
    query_grad[...] = grad_q.astype(BF)
    if not first:
        key_part = key_part + before[0]
        value_part = value_part + before[1]
    acc[0] = key_part.astype(acc.dtype)
    acc[1] = value_part.astype(acc.dtype)


def weight_body(own, idx, whole, grad, keep, send):
    for out, core in ((keep, 0), (send, 1)):
        for a in range(2):
            k = (idx[1] ^ (core + 2 * a)) ^ idx[0]
            for s in range(2):
                out[a, :, s * own : (s + 1) * own] = dot(whole[k, s * KP : (s + 1) * KP, :], grad[s], 0, 0)


def arrange_body(own, idx, w_own, w_core, out):
    part = w_own.shape[2]
    for c, w in enumerate((w_own, w_core)):
        for a in range(w.shape[0]):
            row = pl.multiple_of((idx[2 + a] ^ c) * part, part)
            for k in range(w.shape[1]):
                for s in range(2):
                    out[s, pl.ds(row, part), k * own : (k + 1) * own] = w[a, k, :, s * own : (s + 1) * own]


def tail_body(nd, idx, *rest):
    grads, (w, e, x, input_grad, length_terms, cg) = rest[:4], rest[4:]
    for s in range(2):
        grad = jnp.concatenate([part[s] for part in grads], axis=1)
        cg[s * KP : (s + 1) * KP, :] = dot(grad, w[s], 1, 1).astype(BF)
    both = cg[...]
    terms = dot(x[...], both, 1, 1)
    rows = x.shape[0] // nd
    for a in range(nd):
        length_terms[idx[1] ^ a] = terms[a * rows : (a + 1) * rows, :]
    input_grad[...] = dot(e[...], both, 1, 0).astype(BF)


def place_body(n, own, idx, *rest):
    out = rest[n]
    for k in range(n):
        col = pl.multiple_of((idx[0] ^ k) * own, own)
        out[:, pl.ds(col, own)] = rest[k][...]


def by_heads(ng, n, nd, inputs, queries, cotangent, length_proj, key_value_weight):
    tokens, query_rows, grad_rows = inputs[0], queries[0], cotangent[0]
    rows, width = tokens.shape
    own = width // n
    plane = ng * nd
    g, i, d = lax.axis_index("groups"), lax.axis_index("ctx"), lax.axis_index("dp")
    m = g * nd + d
    flips = [(gy, dx) for gy in range(2) for dx in range(2)]
    idx = jnp.stack([i, d] + [(g ^ gy) * nd + (d ^ (2 * dx)) for gy, dx in flips]).astype(jnp.int32)

    def swap(axis_size, a):
        return [(j, j ^ a) for j in range(axis_size)]

    def to_line(x, k):
        return lax.ppermute(x, "ctx", swap(n, k))

    def over_line(x):
        side = to_line(x, 1)
        near = jnp.stack(
            [lax.ppermute(x, "ctx", [(1, 2), (2, 1)]), lax.ppermute(x, "ctx", [(0, 2), (3, 1)])]
        )
        far = lax.ppermute(near, "ctx", [(1, 0), (2, 3)])
        return x, side, near, far

    def over_plane(x):
        across = [x]
        for gy, dx in flips[1:]:
            perm = [
                (a * nd + b, (a ^ gy) * nd + (b ^ (2 * dx))) for a in range(ng) for b in range(nd)
            ]
            across.append(lax.ppermute(x, ("groups", "dp"), perm))
        return across

    def over_cores(x):
        return lax.ppermute(x, "dp", swap(nd, 1))

    def join_ends(parts, after, name):
        return call(
            join_ends_body, [shape((n, *parts[0].shape), BF)], [idx, *parts], after, name=name
        )[0]

    def pack_queries(k, after):
        return call(
            functools.partial(pack_pair_body, own, k),
            [shape((2, rows, own), BF)],
            [idx, query_rows, grad_rows],
            after,
            name="pack_queries",
        )[0]

    part = rows // plane
    piece = lax.dynamic_slice_in_dim(length_proj, m * part, part, 0).reshape(part, 2 * KP)
    blocks = call(
        functools.partial(pack_body, n, own), [shape((rows, own), BF)] * n, [idx, tokens], name="pack_inputs"
    )
    pieces = [piece] + [to_line(piece, k) for k in range(1, n)]
    blocks = [blocks[0]] + [to_line(blocks[k], k) for k in range(1, n)]
    line = call(
        join_body, [shape((n, part, 2 * KP), BF)], [idx, *pieces], [blocks[1]], name="join_pieces"
    )[0]
    across = over_plane(line)
    packed3 = pack_queries(3, [line])
    e_own = call(
        join_body, [shape((n, n, part, 2 * KP), BF)], [idx, *across], [*blocks[2:], packed3], name="join_lines"
    )[0]
    packed2 = pack_queries(2, [e_own])
    e_core = over_cores(e_own)
    w = key_value_weight.reshape(width, 2 * own)
    compressed = call(
        functools.partial(compress_body, n, plane, rows),
        [shape((2 * KP, own), BF)],
        [idx, e_own, e_core, *blocks],
        [packed2],
        [pltpu.VMEM((n * rows, 2 * KP), BF)],
        name="compress",
    )[0]
    parts = over_line(compressed)

    packed1 = pack_queries(1, [parts[2]])
    qg = [pack_queries(0, []), to_line(packed1, 1), to_line(packed2, 2), to_line(packed3, 3)]
    w_piece = call(
        slice_body, [shape((width // plane, 2 * own), BF)], [idx, w], [parts[1]], name="slice_weight"
    )[0]
    w_line = join_ends(over_line(w_piece), [], "join_weight")
    keys, values, whole = call(
        functools.partial(project_body, own),
        [shape((KP, own), BF)] * 2 + [shape((n, 2 * KP, own), BF)],
        [idx, *parts, w],
        [qg[2], packed1, w_line],
        name="project",
    )

    heads = own // DH
    query_grads, acc = {}, None
    order = (0, 2, 3, 1)
    for k in order:
        first, last = k == order[0], k == order[-1]
        query_grads[k], acc = call(
            functools.partial(attention_body, heads, first, last),
            [shape((rows, own), BF), shape((2, KP, own), BF if last else F32)],
            [idx, keys, values, qg[k]] + ([] if first else [acc]),
            name="attention",
        )
    grads = [acc] + [to_line(acc, k) for k in range(1, n)]

    keep, send = call(
        functools.partial(weight_body, own),
        [shape((2, width // nd, 2 * own), F32)] * 2,
        [idx, whole, acc],
        name="weight",
    )
    w_across = over_plane(w_line)
    w_own = call(
        join_body, [shape((n, n, width // plane, 2 * own), BF)], [idx, *w_across], [keep, grads[1], grads[2]], name="join_weights"
    )[0]
    w_core = over_cores(w_own)
    w_all = call(
        functools.partial(arrange_body, own),
        [shape((2, width, width), BF)],
        [idx, w_own, w_core],
        [grads[2]],
        name="arrange_weight",
    )[0]

    pair = keep + lax.ppermute(send, "dp", swap(nd, 1))
    weight_grad = pair[0] + lax.ppermute(pair[1], "dp", swap(nd, 2))
    weight_grad = weight_grad.reshape(-1, 2, own)

    late = gate([query_grads[k] for k in range(1, n)], [grads[2]], "hold_query_grads")
    returned = [query_grads[0]] + [to_line(late[k - 1], k) for k in range(1, n)]

    input_grad, terms = call(
        functools.partial(tail_body, nd),
        [shape((rows, width), BF), shape((nd, rows // nd, 2 * KP), F32)],
        [idx, *grads, w_all, length_proj.reshape(rows, 2 * KP), tokens],
        [],
        [pltpu.VMEM((2 * KP, width), BF)],
        name="tail",
    )
    length_grad = terms[0]
    for a in range(1, nd):
        length_grad = length_grad + lax.ppermute(terms[a], "dp", swap(nd, a))
    length_grad = length_grad.reshape(-1, 2, KP)

    query_grad = call(
        functools.partial(place_body, n, own),
        [shape((rows, width), BF)],
        [idx, *returned],
        [terms],
        name="place",
    )[0]
    return query_grad[None], input_grad[None], length_grad, weight_grad


def by_positions(inputs, queries, cotangent, length_proj, key_value_weight):
    scale = DH ** (-0.5)
    tokens = inputs[0]
    query_row_block = queries[0]
    grad_rows = cotangent[0]
    rows = tokens.shape[0]
    full_width = key_value_weight.shape[0]
    compress = jnp.einsum("lsk,ld->skd", length_proj, tokens, preferred_element_type=jnp.float32)
    length_compressed = lax.psum(compress, "ctx").astype(jnp.bfloat16)
    own_proj = jnp.einsum(
        "skd,dsc->skc", length_compressed, key_value_weight, preferred_element_type=jnp.float32
    ).astype(jnp.bfloat16)
    length_projected = lax.all_gather(own_proj, "ctx", axis=2, tiled=True)
    keys = length_projected[0].reshape(KP, HEADS, DH)
    values = length_projected[1].reshape(KP, HEADS, DH)
    query_heads = query_row_block.reshape(rows, HEADS, DH)
    grad_heads = grad_rows.reshape(rows, HEADS, DH)
    scores = (
        jnp.einsum("lhd,khd->hlk", query_heads, keys, preferred_element_type=jnp.float32) * scale
    )
    probs = jax.nn.softmax(scores, axis=-1)
    probs_low = probs.astype(jnp.bfloat16)
    dprobs = jnp.einsum("lhd,khd->hlk", grad_heads, values, preferred_element_type=jnp.float32)
    delta = jnp.sum(probs * dprobs, axis=-1, keepdims=True)
    dscores = (probs * (dprobs - delta) * scale).astype(jnp.bfloat16)
    query_grad = jnp.einsum(
        "hlk,khd->lhd", dscores, keys, preferred_element_type=jnp.float32
    ).astype(jnp.bfloat16)
    query_grad = query_grad.reshape(1, rows, full_width)
    key_part = jnp.einsum("hlk,lhd->khd", dscores, query_heads, preferred_element_type=jnp.float32)
    value_part = jnp.einsum(
        "hlk,lhd->khd", probs_low, grad_heads, preferred_element_type=jnp.float32
    )
    partial_grad = jnp.stack([key_part.reshape(KP, full_width), value_part.reshape(KP, full_width)])
    own_grad = lax.psum_scatter(partial_grad, "ctx", scatter_dimension=2, tiled=True).astype(
        jnp.bfloat16
    )
    grad_term = jnp.einsum(
        "skc,dsc->skd", own_grad, key_value_weight, preferred_element_type=jnp.float32
    )
    compression_gradient = lax.psum(grad_term, "ctx").astype(jnp.bfloat16)
    input_grad = jnp.einsum(
        "lsk,skd->ld", length_proj, compression_gradient, preferred_element_type=jnp.float32
    ).astype(jnp.bfloat16)
    input_grad = input_grad.reshape(1, rows, full_width)
    length_grad = lax.psum_scatter(
        jnp.einsum("ld,skd->lsk", tokens, compression_gradient, preferred_element_type=jnp.float32),
        "dp",
        scatter_dimension=0,
        tiled=True,
    )
    weight_grad = lax.psum_scatter(
        jnp.einsum("skd,skc->dsc", length_compressed, own_grad, preferred_element_type=jnp.float32),
        "dp",
        scatter_dimension=0,
        tiled=True,
    )
    return (query_grad, input_grad, length_grad, weight_grad)


def solution(mesh):
    ng, n, nd = (mesh.shape[a] for a in ("groups", "ctx", "dp"))

    def local(*args):
        rows, width = args[0].shape[1:]
        fits = ng == 2 and n == 4 and nd == 4 and width % (n * 128) == 0 and HEADS % n == 0 and rows % 128 == 0
        if fits:
            return by_heads(ng, n, nd, *args)
        return by_positions(*args)

    in_specs = (
        P(("groups", "dp"), "ctx", None),
        P(("groups", "dp"), "ctx", None),
        P(("groups", "dp"), "ctx", None),
        P("ctx", None, None),
        P(None, None, "ctx"),
    )
    out_specs = (
        P(("groups", "dp"), "ctx", None),
        P(("groups", "dp"), "ctx", None),
        P(("groups", "ctx", "dp"), None, None),
        P(("groups", "dp"), None, "ctx"),
    )
    return jax.shard_map(local, mesh=mesh, in_specs=in_specs, out_specs=out_specs, check_vma=False)
```

```python
import functools

import jax
import jax.numpy as jnp
from jax import lax
from jax.experimental import pallas as pl
from jax.experimental.pallas import tpu as pltpu
from jax.sharding import PartitionSpec as P

HEADS = 16
DH = 64
KP = 256
BF = jnp.bfloat16
OPT = {'farsplit': 0, 'att': 'blocks', 'wz': 'relay', 'wslice': 'side', 'wreq': 'project', 'preq': 'two', 'jw': 'g12', 'rs': 'direct', 'agp': 'direct', 'late': 'g2', 'p1': 'line', 'p3': 'line2'}
F32 = jnp.float32
VMEM_LIMIT = 24 * 1024 * 1024


def dot(a, b, ca, cb):
    return lax.dot_general(a, b, (((ca,), (cb,)), ((), ())), preferred_element_type=F32)


def call(body, outs, args, after=(), scratch=(), name=None):
    vmem = pl.BlockSpec(memory_space=pltpu.VMEM)

    def run(*refs):
        body(*refs[: len(args)], *refs[len(args) + len(after) :])

    return pl.pallas_call(
        run,
        out_shape=outs,
        in_specs=[pl.BlockSpec(memory_space=pltpu.SMEM)]
        + [vmem] * (len(args) - 1)
        + [pl.BlockSpec(memory_space=pl.ANY)] * len(after),
        out_specs=[vmem] * len(outs),
        scratch_shapes=list(scratch),
        compiler_params=pltpu.CompilerParams(vmem_limit_bytes=VMEM_LIMIT),
        cost_estimate=pl.CostEstimate(flops=1, bytes_accessed=1, transcendentals=0),
        name=name,
    )(*args, *after)


def gate(arrays, after, name):
    return pl.pallas_call(
        lambda *refs: None,
        out_shape=[shape(a.shape, a.dtype) for a in arrays],
        in_specs=[pl.BlockSpec(memory_space=pl.ANY)] * (len(arrays) + len(after)),
        out_specs=[pl.BlockSpec(memory_space=pl.ANY)] * len(arrays),
        input_output_aliases={k: k for k in range(len(arrays))},
        cost_estimate=pl.CostEstimate(flops=1, bytes_accessed=1, transcendentals=0),
        name=name,
    )(*arrays, *after)


def shape(dims, dtype):
    return jax.ShapeDtypeStruct(dims, dtype)


def pack_body(n, own, idx, *rest):
    x, outs = rest[0], rest[1:]
    for k in range(n):
        col = pl.multiple_of((idx[0] ^ k) * own, own)
        outs[k][...] = x[:, pl.ds(col, own)]


def pack_pair_body(own, k, idx, q, g, out):
    col = pl.multiple_of((idx[0] ^ k) * own, own)
    out[0] = q[:, pl.ds(col, own)]
    out[1] = g[:, pl.ds(col, own)]


def join_ends_body(idx, mine, side, near, far, out):
    inner = (idx[0] == 1) | (idx[0] == 2)
    out[0] = mine[...]
    out[1] = side[...]
    for a in range(2):
        out[2 + a] = pick(inner, near[1 - a], far[a])


def join_body(idx, *rest):
    out = rest[-1]
    for k, x in enumerate(rest[:-1]):
        out[k] = x[...]


def slice_body(idx, x, out):
    rows = out.shape[0]
    out[...] = x[pl.ds(pl.multiple_of(idx[2] * rows, rows), rows), :]


def compress_body(n, plane, rows, idx, e_own, e_core, *rest):
    blocks, out, e_all = rest[:n], rest[n], rest[n + 1]
    part = rows // plane
    for c, e in enumerate((e_own, e_core)):
        for a in range(plane // 2):
            piece = idx[2 + a] ^ c
            for k in range(n):
                row = pl.multiple_of(k * rows + piece * part, 16)
                e_all[pl.ds(row, part), :] = e[a, k]
    total = dot(e_all[0:rows, :], blocks[0][...], 0, 0)
    for k in range(1, n):
        total += dot(e_all[k * rows : (k + 1) * rows, :], blocks[k][...], 0, 0)
    out[...] = total.astype(BF)


def pick(inner, near, far):
    return jnp.where(inner, near, far)


def project_body(own, idx, mine, side, near, far, w, keys, values, whole):
    inner = (idx[0] == 1) | (idx[0] == 2)
    whole[0] = mine[...]
    whole[1] = side[...]
    for a in range(2):
        whole[2 + a] = pick(inner, near[1 - a], far[a])
    for s, out in enumerate((keys, values)):
        total = None
        for k in range(4):
            row = pl.multiple_of((idx[0] ^ k) * own, own)
            term = dot(whole[k, s * KP : (s + 1) * KP, :], w[pl.ds(row, own), s * own : (s + 1) * own], 1, 0)
            total = term if total is None else total + term
        out[...] = total.astype(BF)


def attention_body(heads, first, last, idx, keys, values, qg, *rest):
    if first:
        query_grad, acc = rest
    else:
        before, query_grad, acc = rest
    q, g, kk, vv = qg[0], qg[1], keys[...], values[...]
    scale = DH**-0.5
    lane = lax.broadcasted_iota(jnp.int32, kk.shape, 1)
    grad_q = key_part = value_part = None
    for h in range(heads):
        mask = (lane >= h * DH) & (lane < (h + 1) * DH)
        k_h = jnp.where(mask, kk, jnp.zeros_like(kk))
        v_h = jnp.where(mask, vv, jnp.zeros_like(vv))
        scores = dot(k_h, q, 1, 1)
        e = jnp.exp((scores - jnp.max(scores, axis=0, keepdims=True)) * scale)
        p = e * (1.0 / jnp.sum(e, axis=0, keepdims=True))
        dp = dot(v_h, g, 1, 1)
        delta = jnp.sum(p * dp, axis=0, keepdims=True)
        ds = (p * (dp - delta) * scale).astype(BF)
        term_q = dot(ds, k_h, 0, 0)
        term_k = jnp.where(mask, dot(ds, q, 1, 0), 0.0)
        term_v = jnp.where(mask, dot(p.astype(BF), g, 1, 0), 0.0)
        grad_q = term_q if h == 0 else grad_q + term_q
        key_part = term_k if h == 0 else key_part + term_k
        value_part = term_v if h == 0 else value_part + term_v
    query_grad[...] = grad_q.astype(BF)
    if not first:
        key_part = key_part + before[0]
        value_part = value_part + before[1]
    acc[0] = key_part.astype(acc.dtype)
    acc[1] = value_part.astype(acc.dtype)


def halves_body(n, half, idx, keys, values, *rest):
    pairs, outs, (out, q_all, g_all, p_all, ds_all) = rest[:n], rest[n : 2 * n], rest[2 * n :]
    rows = pairs[0].shape[1]
    width = out.shape[2]
    cols = slice(half * width, (half + 1) * width)
    kk, vv = keys[:, cols], values[:, cols]
    for k in range(n):
        q_all[k * rows : (k + 1) * rows, :] = pairs[k][0, :, cols]
        g_all[k * rows : (k + 1) * rows, :] = pairs[k][1, :, cols]
    scale = DH**-0.5
    lane = lax.broadcasted_iota(jnp.int32, kk.shape, 1)
    grad_q = [None] * n
    key_part = value_part = None
    for h in range(width // DH):
        mask = (lane >= h * DH) & (lane < (h + 1) * DH)
        k_h = jnp.where(mask, kk, jnp.zeros_like(kk))
        v_h = jnp.where(mask, vv, jnp.zeros_like(vv))
        for k in range(n):
            block = slice(k * rows, (k + 1) * rows)
            scores = dot(k_h, q_all[block, :], 1, 1)
            e = jnp.exp((scores - jnp.max(scores, axis=0, keepdims=True)) * scale)
            p = e * (1.0 / jnp.sum(e, axis=0, keepdims=True))
            dp = dot(v_h, g_all[block, :], 1, 1)
            delta = jnp.sum(p * dp, axis=0, keepdims=True)
            ds = (p * (dp - delta) * scale).astype(BF)
            p_all[:, block] = p.astype(BF)
            ds_all[:, block] = ds
            term = dot(ds, k_h, 0, 0)
            grad_q[k] = term if h == 0 else grad_q[k] + term
        term_k = jnp.where(mask, dot(ds_all[...], q_all[...], 1, 0), 0.0)
        term_v = jnp.where(mask, dot(p_all[...], g_all[...], 1, 0), 0.0)
        key_part = term_k if h == 0 else key_part + term_k
        value_part = term_v if h == 0 else value_part + term_v
    for k in range(n):
        outs[k][...] = grad_q[k].astype(BF)
    out[0] = key_part.astype(BF)
    out[1] = value_part.astype(BF)


def weight_body(own, nacc, idx, whole, *rest):
    accs, outs = rest[:nacc], rest[nacc:]
    for a, out in enumerate(outs):
        k = (idx[1] ^ a) ^ idx[0]
        for s in range(2):
            grad = jnp.concatenate([x[s] for x in accs], axis=1) if nacc > 1 else accs[0][s]
            out[:, s * own : (s + 1) * own] = dot(whole[k, s * KP : (s + 1) * KP, :], grad, 0, 0)


def weight_pairs_body(own, nacc, idx, whole, *rest):
    accs, (keep, send) = rest[:nacc], rest[nacc:]
    for out, core in ((keep, 0), (send, 1)):
        for a in range(2):
            k = (idx[1] ^ (core + 2 * a)) ^ idx[0]
            for s in range(2):
                grad = jnp.concatenate([x[s] for x in accs], axis=1) if nacc > 1 else accs[0][s]
                out[a, :, s * own : (s + 1) * own] = dot(whole[k, s * KP : (s + 1) * KP, :], grad, 0, 0)


def arrange_body(own, idx, w_own, w_core, out):
    part = w_own.shape[2]
    for c, w in enumerate((w_own, w_core)):
        for a in range(w.shape[0]):
            row = pl.multiple_of((idx[2 + a] ^ c) * part, part)
            for k in range(w.shape[1]):
                for s in range(2):
                    out[s, pl.ds(row, part), k * own : (k + 1) * own] = w[a, k, :, s * own : (s + 1) * own]


def tail_body(nd, idx, *rest):
    grads, (w, e, x, length_terms, input_grad, cg) = rest[:-6], rest[-6:]
    for s in range(2):
        grad = jnp.concatenate([part[s] for part in grads], axis=1)
        cg[s * KP : (s + 1) * KP, :] = dot(grad, w[s], 1, 1).astype(BF)
    both = cg[...]
    terms = dot(x[...], both, 1, 1)
    rows = x.shape[0] // nd
    for a in range(nd):
        length_terms[idx[1] ^ a] = terms[a * rows : (a + 1) * rows, :]
    input_grad[...] = dot(e[...], both, 1, 0).astype(BF)


def place_body(n, own, idx, *rest):
    out = rest[-1]
    parts = (len(rest) - 1) // n
    width = own // parts
    for k in range(n):
        col = pl.multiple_of((idx[0] ^ k) * own, own)
        for a in range(parts):
            out[:, pl.ds(col + a * width, width)] = rest[k * parts + a][...]


def by_heads(ng, n, nd, inputs, queries, cotangent, length_proj, key_value_weight):
    tokens, query_rows, grad_rows = inputs[0], queries[0], cotangent[0]
    rows, width = tokens.shape
    own = width // n
    plane = ng * nd
    g, i, d = lax.axis_index("groups"), lax.axis_index("ctx"), lax.axis_index("dp")
    m = g * nd + d
    flips = [(gy, dx) for gy in range(2) for dx in range(2)]
    idx = jnp.stack([i, d] + [(g ^ gy) * nd + (d ^ (2 * dx)) for gy, dx in flips]).astype(jnp.int32)

    def swap(axis_size, a):
        return [(j, j ^ a) for j in range(axis_size)]

    def to_line(x, k):
        return lax.ppermute(x, "ctx", swap(n, k))

    def over_line(x):
        side = to_line(x, 1)
        near = jnp.stack(
            [lax.ppermute(x, "ctx", [(1, 2), (2, 1)]), lax.ppermute(x, "ctx", [(0, 2), (3, 1)])]
        )
        if OPT["farsplit"]:
            far = jnp.stack([lax.ppermute(near[a], "ctx", [(1, 0), (2, 3)]) for a in range(2)])
        else:
            far = lax.ppermute(near, "ctx", [(1, 0), (2, 3)])
        return x, side, near, far

    def over_plane(x):
        across = [x]
        for gy, dx in flips[1:]:
            perm = [
                (a * nd + b, (a ^ gy) * nd + (b ^ (2 * dx))) for a in range(ng) for b in range(nd)
            ]
            across.append(lax.ppermute(x, ("groups", "dp"), perm))
        return across

    def over_cores(x):
        return lax.ppermute(x, "dp", swap(nd, 1))

    def join_ends(parts, after, name):
        return call(
            join_ends_body, [shape((n, *parts[0].shape), BF)], [idx, *parts], after, name=name
        )[0]

    def pack_queries(k, after):
        return call(
            functools.partial(pack_pair_body, own, k),
            [shape((2, rows, own), BF)],
            [idx, query_rows, grad_rows],
            after,
            name="pack_queries",
        )[0]

    part = rows // plane
    piece = lax.dynamic_slice_in_dim(length_proj, m * part, part, 0).reshape(part, 2 * KP)
    blocks = call(
        functools.partial(pack_body, n, own), [shape((rows, own), BF)] * n, [idx, tokens], name="pack_inputs"
    )
    pieces = [piece] + [to_line(piece, k) for k in range(1, n)]
    blocks = [blocks[0]] + [to_line(blocks[k], k) for k in range(1, n)]
    line = call(
        join_body, [shape((n, part, 2 * KP), BF)], [idx, *pieces], [blocks[1]], name="join_pieces"
    )[0]
    across = over_plane(line)
    o = OPT
    packed3 = pack_queries(3, [line]) if o["p3"] == "line" else None
    packed1 = pack_queries(1, [line]) if o["p1"] == "line" else None
    packed2 = pack_queries(2, [line]) if o["p3"] == "line2" else None
    e_own = call(
        join_body,
        [shape((n, n, part, 2 * KP), BF)],
        [idx, *across],
        [*blocks[2:], *[p for p in (packed1, packed2, packed3) if p is not None]],
        name="join_lines",
    )[0]
    if packed3 is None:
        packed3 = pack_queries(3, [e_own])
    if packed2 is None:
        packed2 = pack_queries(2, [e_own])
    if packed1 is None and o["p1"] == "e":
        packed1 = pack_queries(1, [e_own])
    e_core = over_cores(e_own)
    w = key_value_weight.reshape(width, 2 * own)
    w_rows = width // plane

    def slice_weight(after):
        return call(slice_body, [shape((w_rows, 2 * own), BF)], [idx, w], after, name="slice_weight")[0]

    w_piece = slice_weight([e_own]) if o["wslice"] == "e" else None
    compressed = call(
        functools.partial(compress_body, n, plane, rows),
        [shape((2 * KP, own), BF)],
        [idx, e_own, e_core, *blocks],
        [p for p in (packed1, packed2, packed3, w_piece) if p is not None],
        [pltpu.VMEM((n * rows, 2 * KP), BF)],
        name="compress",
    )[0]
    parts = over_line(compressed)
    if packed1 is None:
        packed1 = pack_queries(1, [parts[2]])
    qg = [pack_queries(0, []), to_line(packed1, 1), to_line(packed2, 2), to_line(packed3, 3)]
    if w_piece is None:
        gates = dict(side=parts[1], c=compressed, near=parts[2], far=parts[3], q2=qg[2])
        w_piece = slice_weight([gates[o["wslice"]]])
    if o["wz"] == "relay":
        w_parts = over_line(w_piece)

        def join_weight(after):
            return join_ends(w_parts, after, "join_weight")
    else:
        w_parts = [w_piece] + [to_line(w_piece, k) for k in range(1, n)]

        def join_weight(after):
            return call(join_body, [shape((n, w_rows, 2 * own), BF)], [idx, *w_parts], after, name="join_weight")[0]

    w_line = join_weight([]) if o["wreq"] != "late" else None
    req = dict(two=[qg[2], packed1], all=qg[1:], none=[packed1], q12=[qg[1], qg[2]], q23=[qg[2], qg[3]])[o["preq"]]
    keys, values, whole = call(
        functools.partial(project_body, own),
        [shape((KP, own), BF)] * 2 + [shape((n, 2 * KP, own), BF)],
        [idx, *parts, w],
        [*req, *([w_line] if o["wreq"] == "project" else [])],
        name="project",
    )
    if w_line is None:
        w_line = join_weight([keys])

    heads = own // DH
    accs = []
    if o["att"] == "halves":
        query_grads = []
        for half in range(2):
            *parts_q, acc = call(
                functools.partial(halves_body, n, half),
                [shape((rows, own // 2), BF)] * n + [shape((2, KP, own // 2), BF)],
                [idx, keys, values, *qg],
                [accs[0]] if half else [],
                scratch=[pltpu.VMEM((n * rows, own // 2), BF)] * 2 + [pltpu.VMEM((KP, n * rows), BF)] * 2,
                name="attention",
            )
            query_grads.append(parts_q)
            accs.append(acc)
    elif o["att"] == "single":
        *parts_q, acc = call(
            functools.partial(halves_body, n, 0),
            [shape((rows, own), BF)] * n + [shape((2, KP, own), BF)],
            [idx, keys, values, *qg],
            scratch=[pltpu.VMEM((n * rows, own), BF)] * 2 + [pltpu.VMEM((KP, n * rows), BF)] * 2,
            name="attention",
        )
        query_grads = [parts_q]
        accs.append(acc)
    else:
        order, by_block, acc = o.get("order", (0, 2, 3, 1)), {}, None
        for k in order:
            first, last = k == order[0], k == order[-1]
            by_block[k], acc = call(
                functools.partial(attention_body, heads, first, last),
                [shape((rows, own), BF), shape((2, KP, own), BF if last else F32)],
                [idx, keys, values, qg[k]] + ([] if first else [acc]),
                name="attention",
            )
        query_grads = [[by_block[k] for k in range(n)]]
        accs.append(acc)
    na = len(accs)
    grads = []
    for a, acc in enumerate(accs):
        if o["agp"] == "relay" or (o["agp"] == "mixed" and a == 0):
            g_parts = over_line(acc)
            inner = jnp.logical_or(i == 1, i == 2)
            grads.append([acc, g_parts[1], jnp.where(inner, g_parts[2][1], g_parts[3][0]), jnp.where(inner, g_parts[2][0], g_parts[3][1])])
        else:
            grads.append([acc] + [to_line(acc, k) for k in range(1, n)])

    if o["rs"] == "two":
        keep, send = call(
            functools.partial(weight_pairs_body, own, na),
            [shape((2, width // nd, 2 * own), F32)] * 2,
            [idx, whole, *accs],
            name="weight",
        )
        pair = keep + lax.ppermute(send, "dp", swap(nd, 1))
        weight_grad = pair[0] + lax.ppermute(pair[1], "dp", swap(nd, 2))
    else:
        weight = call(
            functools.partial(weight_body, own, na),
            [shape((width // nd, 2 * own), F32)] * nd,
            [idx, whole, *accs],
            [grads[-1][1]] if o["rs"] == "late" else [],
            name="weight",
        )
        keep = weight[0]
        weight_grad = weight[0]
        for a in range(1, nd):
            weight_grad = weight_grad + lax.ppermute(weight[a], "dp", swap(nd, a))
    weight_grad = weight_grad.reshape(-1, 2, own)

    last = grads[-1]
    jw = dict(
        g12=[keep, last[1], last[2]],
        g1=[keep, last[1]],
        g0=[keep, *grads[0][1:]],
        g0l=[keep, *grads[0][1:], last[1], last[2]],
        gall=[keep, *grads[0][1:], *last[1:]],
        keys=[keys],
        acc=[keep],
    )[o["jw"]]
    w_across = over_plane(w_line)
    w_own = call(
        join_body, [shape((n, n, w_rows, 2 * own), BF)], [idx, *w_across], jw, name="join_weights"
    )[0]
    w_core = over_cores(w_own)
    w_all = call(
        functools.partial(arrange_body, own),
        [shape((2, width, width), BF)],
        [idx, w_own, w_core],
        [keep, last[1]],
        name="arrange_weight",
    )[0]

    gate_on = dict(g2=[last[2]], g1=[last[1]], g3=[last[3]], none=[])[o["late"]]
    flat = [x for parts_q in query_grads for x in parts_q[1:]]
    late = gate(flat, gate_on, "hold_query_grads") if gate_on else flat
    returned = []
    for k in range(n):
        for a in range(na):
            returned.append(to_line(late[a * (n - 1) + k - 1], k) if k else query_grads[a][0])

    tail_in = [idx, *(grads[a][k] for k in range(n) for a in range(na)), w_all, length_proj.reshape(rows, 2 * KP), tokens]
    terms, input_grad = call(
        functools.partial(tail_body, nd),
        [shape((nd, rows // nd, 2 * KP), F32), shape((rows, width), BF)],
        tail_in,
        scratch=[pltpu.VMEM((2 * KP, width), BF)],
        name="tail",
    )
    length_grad = terms[0]
    for a in range(1, nd):
        length_grad = length_grad + lax.ppermute(terms[a], "dp", swap(nd, a))
    length_grad = length_grad.reshape(-1, 2, KP)

    query_grad = call(
        functools.partial(place_body, n, own),
        [shape((rows, width), BF)],
        [idx, *returned],
        [terms],
        name="place",
    )[0]
    return query_grad[None], input_grad[None], length_grad, weight_grad


def by_positions(inputs, queries, cotangent, length_proj, key_value_weight):
    scale = DH ** (-0.5)
    tokens = inputs[0]
    query_row_block = queries[0]
    grad_rows = cotangent[0]
    rows = tokens.shape[0]
    full_width = key_value_weight.shape[0]
    compress = jnp.einsum("lsk,ld->skd", length_proj, tokens, preferred_element_type=jnp.float32)
    length_compressed = lax.psum(compress, "ctx").astype(jnp.bfloat16)
    own_proj = jnp.einsum(
        "skd,dsc->skc", length_compressed, key_value_weight, preferred_element_type=jnp.float32
    ).astype(jnp.bfloat16)
    length_projected = lax.all_gather(own_proj, "ctx", axis=2, tiled=True)
    keys = length_projected[0].reshape(KP, HEADS, DH)
    values = length_projected[1].reshape(KP, HEADS, DH)
    query_heads = query_row_block.reshape(rows, HEADS, DH)
    grad_heads = grad_rows.reshape(rows, HEADS, DH)
    scores = (
        jnp.einsum("lhd,khd->hlk", query_heads, keys, preferred_element_type=jnp.float32) * scale
    )
    probs = jax.nn.softmax(scores, axis=-1)
    probs_low = probs.astype(jnp.bfloat16)
    dprobs = jnp.einsum("lhd,khd->hlk", grad_heads, values, preferred_element_type=jnp.float32)
    delta = jnp.sum(probs * dprobs, axis=-1, keepdims=True)
    dscores = (probs * (dprobs - delta) * scale).astype(jnp.bfloat16)
    query_grad = jnp.einsum(
        "hlk,khd->lhd", dscores, keys, preferred_element_type=jnp.float32
    ).astype(jnp.bfloat16)
    query_grad = query_grad.reshape(1, rows, full_width)
    key_part = jnp.einsum("hlk,lhd->khd", dscores, query_heads, preferred_element_type=jnp.float32)
    value_part = jnp.einsum(
        "hlk,lhd->khd", probs_low, grad_heads, preferred_element_type=jnp.float32
    )
    partial_grad = jnp.stack([key_part.reshape(KP, full_width), value_part.reshape(KP, full_width)])
    own_grad = lax.psum_scatter(partial_grad, "ctx", scatter_dimension=2, tiled=True).astype(
        jnp.bfloat16
    )
    grad_term = jnp.einsum(
        "skc,dsc->skd", own_grad, key_value_weight, preferred_element_type=jnp.float32
    )
    compression_gradient = lax.psum(grad_term, "ctx").astype(jnp.bfloat16)
    input_grad = jnp.einsum(
        "lsk,skd->ld", length_proj, compression_gradient, preferred_element_type=jnp.float32
    ).astype(jnp.bfloat16)
    input_grad = input_grad.reshape(1, rows, full_width)
    length_grad = lax.psum_scatter(
        jnp.einsum("ld,skd->lsk", tokens, compression_gradient, preferred_element_type=jnp.float32),
        "dp",
        scatter_dimension=0,
        tiled=True,
    )
    weight_grad = lax.psum_scatter(
        jnp.einsum("skd,skc->dsc", length_compressed, own_grad, preferred_element_type=jnp.float32),
        "dp",
        scatter_dimension=0,
        tiled=True,
    )
    return (query_grad, input_grad, length_grad, weight_grad)


def solution(mesh):
    ng, n, nd = (mesh.shape[a] for a in ("groups", "ctx", "dp"))

    def local(*args):
        rows, width = args[0].shape[1:]
        fits = ng == 2 and n == 4 and nd == 4 and width % (n * 128) == 0 and HEADS % n == 0 and rows % 128 == 0
        if fits:
            return by_heads(ng, n, nd, *args)
        return by_positions(*args)

    in_specs = (
        P(("groups", "dp"), "ctx", None),
        P(("groups", "dp"), "ctx", None),
        P(("groups", "dp"), "ctx", None),
        P("ctx", None, None),
        P(None, None, "ctx"),
    )
    out_specs = (
        P(("groups", "dp"), "ctx", None),
        P(("groups", "dp"), "ctx", None),
        P(("groups", "ctx", "dp"), None, None),
        P(("groups", "dp"), None, "ctx"),
    )
    return jax.shard_map(local, mesh=mesh, in_specs=in_specs, out_specs=out_specs, check_vma=False)
```

```python
import functools

import jax
import jax.numpy as jnp
from jax import lax
from jax.experimental import pallas as pl
from jax.experimental.pallas import tpu as pltpu
from jax.sharding import PartitionSpec as P

HEADS = 16
DH = 64
KP = 256
BF = jnp.bfloat16
OPT = {'farsplit': 0, 'att': 'single', 'wz': 'direct', 'wslice': 'side', 'wreq': 'project', 'preq': 'two', 'jw': 'g12', 'rs': 'direct', 'agp': 'direct', 'late': 'none', 'p1': 'line', 'p3': 'line2', 'q1': 'no', 'sum': 'pallas', 'pad': 0, 'ws': 'none', 'lq': 0, 'nq': 1, 'pad2': 0, 'xj': 0, 'order': 'b0231'}
F32 = jnp.float32
VMEM_LIMIT = 24 * 1024 * 1024


def dot(a, b, ca, cb):
    return lax.dot_general(a, b, (((ca,), (cb,)), ((), ())), preferred_element_type=F32)


def call(body, outs, args, after=(), scratch=(), name=None):
    vmem = pl.BlockSpec(memory_space=pltpu.VMEM)

    def run(*refs):
        body(*refs[: len(args)], *refs[len(args) + len(after) :])

    return pl.pallas_call(
        run,
        out_shape=outs,
        in_specs=[pl.BlockSpec(memory_space=pltpu.SMEM)]
        + [vmem] * (len(args) - 1)
        + [pl.BlockSpec(memory_space=pl.ANY)] * len(after),
        out_specs=[vmem] * len(outs),
        scratch_shapes=list(scratch),
        compiler_params=pltpu.CompilerParams(vmem_limit_bytes=VMEM_LIMIT),
        cost_estimate=pl.CostEstimate(flops=1, bytes_accessed=1, transcendentals=0),
        name=name,
    )(*args, *after)


def gate(arrays, after, name):
    return pl.pallas_call(
        lambda *refs: None,
        out_shape=[shape(a.shape, a.dtype) for a in arrays],
        in_specs=[pl.BlockSpec(memory_space=pl.ANY)] * (len(arrays) + len(after)),
        out_specs=[pl.BlockSpec(memory_space=pl.ANY)] * len(arrays),
        input_output_aliases={k: k for k in range(len(arrays))},
        cost_estimate=pl.CostEstimate(flops=1, bytes_accessed=1, transcendentals=0),
        name=name,
    )(*arrays, *after)


def shape(dims, dtype):
    return jax.ShapeDtypeStruct(dims, dtype)


def pack_body(n, own, idx, *rest):
    x, outs = rest[0], rest[1:]
    for k in range(n):
        col = pl.multiple_of((idx[0] ^ k) * own, own)
        outs[k][...] = x[:, pl.ds(col, own)]


def pack_pair_body(own, k, idx, q, g, out):
    col = pl.multiple_of((idx[0] ^ k) * own, own)
    out[0] = q[:, pl.ds(col, own)]
    out[1] = g[:, pl.ds(col, own)]


def join_ends_body(idx, mine, side, near, far, out):
    inner = (idx[0] == 1) | (idx[0] == 2)
    out[0] = mine[...]
    out[1] = side[...]
    for a in range(2):
        out[2 + a] = pick(inner, near[1 - a], far[a])


def join_body(idx, *rest):
    out = rest[-1]
    for k, x in enumerate(rest[:-1]):
        out[k] = x[...]


def slice_body(idx, x, out):
    rows = out.shape[0]
    out[...] = x[pl.ds(pl.multiple_of(idx[2] * rows, rows), rows), :]


def compress_body(n, plane, rows, idx, e_own, e_core, *rest):
    blocks, out, e_all = rest[:n], rest[n], rest[n + 1]
    part = rows // plane
    for c, e in enumerate((e_own, e_core)):
        for a in range(plane // 2):
            piece = idx[2 + a] ^ c
            for k in range(n):
                row = pl.multiple_of(k * rows + piece * part, 16)
                e_all[pl.ds(row, part), :] = e[a, k]
    total = dot(e_all[0:rows, :], blocks[0][...], 0, 0)
    for k in range(1, n):
        total += dot(e_all[k * rows : (k + 1) * rows, :], blocks[k][...], 0, 0)
    out[...] = total.astype(BF)


def pick(inner, near, far):
    return jnp.where(inner, near, far)


def project_body(own, idx, mine, side, near, far, w, keys, values, whole):
    inner = (idx[0] == 1) | (idx[0] == 2)
    whole[0] = mine[...]
    whole[1] = side[...]
    for a in range(2):
        whole[2 + a] = pick(inner, near[1 - a], far[a])
    for s, out in enumerate((keys, values)):
        total = None
        for k in range(4):
            row = pl.multiple_of((idx[0] ^ k) * own, own)
            term = dot(whole[k, s * KP : (s + 1) * KP, :], w[pl.ds(row, own), s * own : (s + 1) * own], 1, 0)
            total = term if total is None else total + term
        out[...] = total.astype(BF)


def attention_body(heads, first, last, idx, keys, values, qg, *rest):
    if first:
        query_grad, acc = rest
    else:
        before, query_grad, acc = rest
    q, g, kk, vv = qg[0], qg[1], keys[...], values[...]
    scale = DH**-0.5
    lane = lax.broadcasted_iota(jnp.int32, kk.shape, 1)
    grad_q = key_part = value_part = None
    for h in range(heads):
        mask = (lane >= h * DH) & (lane < (h + 1) * DH)
        k_h = jnp.where(mask, kk, jnp.zeros_like(kk))
        v_h = jnp.where(mask, vv, jnp.zeros_like(vv))
        scores = dot(k_h, q, 1, 1)
        e = jnp.exp((scores - jnp.max(scores, axis=0, keepdims=True)) * scale)
        p = e * (1.0 / jnp.sum(e, axis=0, keepdims=True))
        dp = dot(v_h, g, 1, 1)
        delta = jnp.sum(p * dp, axis=0, keepdims=True)
        ds = (p * (dp - delta) * scale).astype(BF)
        term_q = dot(ds, k_h, 0, 0)
        term_k = jnp.where(mask, dot(ds, q, 1, 0), 0.0)
        term_v = jnp.where(mask, dot(p.astype(BF), g, 1, 0), 0.0)
        grad_q = term_q if h == 0 else grad_q + term_q
        key_part = term_k if h == 0 else key_part + term_k
        value_part = term_v if h == 0 else value_part + term_v
    rows = grad_q.shape[0]
    query_grad[:rows, :] = grad_q.astype(BF)
    if query_grad.shape[0] > rows:
        query_grad[rows:, :] = jnp.zeros_like(query_grad[rows:, :])
    if not first:
        key_part = key_part + before[0]
        value_part = value_part + before[1]
    acc[0] = key_part.astype(acc.dtype)
    acc[1] = value_part.astype(acc.dtype)


def halves_body(n, half, idx, keys, values, *rest):
    pairs, outs, (out, q_all, g_all, p_all, ds_all) = rest[:n], rest[n : 2 * n], rest[2 * n :]
    rows = pairs[0].shape[1]
    width = out.shape[2]
    cols = slice(half * width, (half + 1) * width)
    kk, vv = keys[:, cols], values[:, cols]
    for k in range(n):
        q_all[k * rows : (k + 1) * rows, :] = pairs[k][0, :, cols]
        g_all[k * rows : (k + 1) * rows, :] = pairs[k][1, :, cols]
    scale = DH**-0.5
    lane = lax.broadcasted_iota(jnp.int32, kk.shape, 1)
    grad_q = [None] * n
    key_part = value_part = None
    for h in range(width // DH):
        mask = (lane >= h * DH) & (lane < (h + 1) * DH)
        k_h = jnp.where(mask, kk, jnp.zeros_like(kk))
        v_h = jnp.where(mask, vv, jnp.zeros_like(vv))
        for k in range(n):
            block = slice(k * rows, (k + 1) * rows)
            scores = dot(k_h, q_all[block, :], 1, 1)
            e = jnp.exp((scores - jnp.max(scores, axis=0, keepdims=True)) * scale)
            p = e * (1.0 / jnp.sum(e, axis=0, keepdims=True))
            dp = dot(v_h, g_all[block, :], 1, 1)
            delta = jnp.sum(p * dp, axis=0, keepdims=True)
            ds = (p * (dp - delta) * scale).astype(BF)
            p_all[:, block] = p.astype(BF)
            ds_all[:, block] = ds
            term = dot(ds, k_h, 0, 0)
            grad_q[k] = term if h == 0 else grad_q[k] + term
        term_k = jnp.where(mask, dot(ds_all[...], q_all[...], 1, 0), 0.0)
        term_v = jnp.where(mask, dot(p_all[...], g_all[...], 1, 0), 0.0)
        key_part = term_k if h == 0 else key_part + term_k
        value_part = term_v if h == 0 else value_part + term_v
    for k in range(n):
        outs[k][...] = grad_q[k].astype(BF)
    out[0] = key_part.astype(BF)
    out[1] = value_part.astype(BF)


def weight_body(own, nacc, idx, whole, *rest):
    accs, outs = rest[:nacc], rest[nacc:]
    for a, out in enumerate(outs):
        k = (idx[1] ^ a) ^ idx[0]
        for s in range(2):
            grad = jnp.concatenate([x[s] for x in accs], axis=1) if nacc > 1 else accs[0][s]
            out[:, s * own : (s + 1) * own] = dot(whole[k, s * KP : (s + 1) * KP, :], grad, 0, 0)


def weight_pairs_body(own, nacc, idx, whole, *rest):
    accs, (keep, send) = rest[:nacc], rest[nacc:]
    for out, core in ((keep, 0), (send, 1)):
        for a in range(2):
            k = (idx[1] ^ (core + 2 * a)) ^ idx[0]
            for s in range(2):
                grad = jnp.concatenate([x[s] for x in accs], axis=1) if nacc > 1 else accs[0][s]
                out[a, :, s * own : (s + 1) * own] = dot(whole[k, s * KP : (s + 1) * KP, :], grad, 0, 0)


def arrange_body(own, idx, w_own, w_core, out):
    part = w_own.shape[2]
    for c, w in enumerate((w_own, w_core)):
        for a in range(w.shape[0]):
            row = pl.multiple_of((idx[2 + a] ^ c) * part, part)
            for k in range(w.shape[1]):
                for s in range(2):
                    out[s, pl.ds(row, part), k * own : (k + 1) * own] = w[a, k, :, s * own : (s + 1) * own]


def tail_body(nd, idx, *rest):
    length_terms, (input_grad, cg, terms) = rest[-3 - nd : -3], rest[-3:]
    grads, (w, e, x) = rest[: -6 - nd], rest[-6 - nd : -3 - nd]
    for s in range(2):
        grad = jnp.concatenate([part[s] for part in grads], axis=1)
        cg[s * KP : (s + 1) * KP, :] = dot(grad, w[s], 1, 1).astype(BF)
    both = cg[...]
    terms[...] = dot(x[...], both, 1, 1)
    rows = x.shape[0] // nd
    for a in range(nd):
        length_terms[a][...] = terms[pl.ds(pl.multiple_of((idx[1] ^ a) * rows, 16), rows), :]
    input_grad[...] = dot(e[...], both, 1, 0).astype(BF)


def sum_body(idx, *rest):
    out = rest[-1]
    total = rest[0][...]
    for x in rest[1:-1]:
        total = total + x[...]
    for s in range(2):
        out[:, s, :] = total[:, s * KP : (s + 1) * KP]


def place_body(n, own, idx, *rest):
    out = rest[-1]
    parts = (len(rest) - 1) // n
    width = own // parts
    for k in range(n):
        col = pl.multiple_of((idx[0] ^ k) * own, own)
        for a in range(parts):
            out[:, pl.ds(col + a * width, width)] = rest[k * parts + a][: out.shape[0], :]


def by_heads(ng, n, nd, inputs, queries, cotangent, length_proj, key_value_weight):
    tokens, query_rows, grad_rows = inputs[0], queries[0], cotangent[0]
    rows, width = tokens.shape
    own = width // n
    plane = ng * nd
    g, i, d = lax.axis_index("groups"), lax.axis_index("ctx"), lax.axis_index("dp")
    m = g * nd + d
    flips = [(gy, dx) for gy in range(2) for dx in range(2)]
    idx = jnp.stack([i, d] + [(g ^ gy) * nd + (d ^ (2 * dx)) for gy, dx in flips]).astype(jnp.int32)

    def swap(axis_size, a):
        return [(j, j ^ a) for j in range(axis_size)]

    def to_line(x, k):
        return lax.ppermute(x, "ctx", swap(n, k))

    def over_line(x, after=()):
        side = to_line(x, 1)
        near = [lax.ppermute(x, "ctx", [(1, 2), (2, 1)]), lax.ppermute(x, "ctx", [(0, 2), (3, 1)])]
        if after:
            near = call(join_body, [shape((2, *x.shape), BF)], [idx, *near], after, name="join_near")[0]
        else:
            near = jnp.stack(near)
        if OPT["farsplit"]:
            far = jnp.stack([lax.ppermute(near[a], "ctx", [(1, 0), (2, 3)]) for a in range(2)])
        else:
            far = lax.ppermute(near, "ctx", [(1, 0), (2, 3)])
        return x, side, near, far

    def over_plane(x):
        across = [x]
        for gy, dx in flips[1:]:
            perm = [
                (a * nd + b, (a ^ gy) * nd + (b ^ (2 * dx))) for a in range(ng) for b in range(nd)
            ]
            across.append(lax.ppermute(x, ("groups", "dp"), perm))
        return across

    def over_cores(x):
        return lax.ppermute(x, "dp", swap(nd, 1))

    def join_ends(parts, after, name):
        return call(
            join_ends_body, [shape((n, *parts[0].shape), BF)], [idx, *parts], after, name=name
        )[0]

    def pack_queries(k, after):
        return call(
            functools.partial(pack_pair_body, own, k),
            [shape((2, rows, own), BF)],
            [idx, query_rows, grad_rows],
            after,
            name="pack_queries",
        )[0]

    part = rows // plane
    piece = lax.dynamic_slice_in_dim(length_proj, m * part, part, 0).reshape(part, 2 * KP)
    blocks = call(
        functools.partial(pack_body, n, own), [shape((rows, own), BF)] * n, [idx, tokens], name="pack_inputs"
    )
    pieces = [piece] + [to_line(piece, k) for k in range(1, n)]
    blocks = [blocks[0]] + [to_line(blocks[k], k) for k in range(1, n)]
    line = call(
        join_body, [shape((n, part, 2 * KP), BF)], [idx, *pieces], [blocks[1]] if OPT["xj"] else [], name="join_pieces"
    )[0]
    across = over_plane(line)
    o = OPT
    packed0 = pack_queries(0, [line])
    packed3 = pack_queries(3, [line]) if o["p3"] == "line" else None
    packed1 = pack_queries(1, [line]) if o["p1"] == "line" else None
    packed2 = pack_queries(2, [line]) if o["p3"] == "line2" else None
    e_own = call(
        join_body,
        [shape((n, n, part, 2 * KP), BF)],
        [idx, *across],
        [*blocks[2:], *[p for p in (packed0, packed1, packed2, packed3) if p is not None]],
        name="join_lines",
    )[0]
    if packed3 is None:
        packed3 = pack_queries(3, [e_own])
    if packed2 is None:
        packed2 = pack_queries(2, [e_own])
    if packed1 is None and o["p1"] == "e":
        packed1 = pack_queries(1, [e_own])
    e_core = over_cores(e_own)
    w = key_value_weight.reshape(width, 2 * own)
    w_rows = width // plane

    def slice_weight(after):
        return call(slice_body, [shape((w_rows, 2 * own), BF)], [idx, w], after, name="slice_weight")[0]

    w_piece = slice_weight([e_own]) if o["wslice"] == "e" else None
    compressed = call(
        functools.partial(compress_body, n, plane, rows),
        [shape((2 * KP, own), BF)],
        [idx, e_own, e_core, *blocks],
        [p for p in (packed1, packed2, packed3, w_piece) if p is not None],
        [pltpu.VMEM((n * rows, 2 * KP), BF)],
        name="compress",
    )[0]
    early = to_line(packed1, 1) if o["nq"] else None
    parts = over_line(compressed, [early] if o["nq"] else [])
    if packed1 is None:
        packed1 = pack_queries(1, [parts[2]])
    qg = [packed0, to_line(packed1, 1) if early is None else early, to_line(packed2, 2), to_line(packed3, 3)]
    if w_piece is None:
        gates = dict(side=parts[1], c=compressed, near=parts[2], far=parts[3], q2=qg[2])
        w_piece = slice_weight([gates[o["wslice"]]])
    if o["wz"] == "relay":
        w_parts = over_line(w_piece)

        def join_weight(after):
            return join_ends(w_parts, after, "join_weight")
    else:
        w_parts = [w_piece] + [to_line(w_piece, k) for k in range(1, n)]

        def join_weight(after):
            return call(join_body, [shape((n, w_rows, 2 * own), BF)], [idx, *w_parts], after, name="join_weight")[0]

    w_line = join_weight([]) if o["wreq"] != "late" else None
    req = dict(two=[qg[2], packed1], all=qg[1:], none=[packed1], q12=[qg[1], qg[2]], q23=[qg[2], qg[3]])[o["preq"]]
    keys, values, whole = call(
        functools.partial(project_body, own),
        [shape((KP, own), BF)] * 2 + [shape((n, 2 * KP, own), BF)],
        [idx, *parts, w],
        [*req, *([w_line] if o["wreq"] == "project" else [])],
        name="project",
    )
    if w_line is None:
        w_line = join_weight([keys])

    heads = own // DH
    accs = []
    if o["att"] == "halves":
        query_grads = []
        for half in range(2):
            *parts_q, acc = call(
                functools.partial(halves_body, n, half),
                [shape((rows, own // 2), BF)] * n + [shape((2, KP, own // 2), BF)],
                [idx, keys, values, *qg],
                [accs[0]] if half else [],
                scratch=[pltpu.VMEM((n * rows, own // 2), BF)] * 2 + [pltpu.VMEM((KP, n * rows), BF)] * 2,
                name="attention",
            )
            query_grads.append(parts_q)
            accs.append(acc)
    elif o["att"] == "single":
        *parts_q, acc = call(
            functools.partial(halves_body, n, 0),
            [shape((rows, own), BF)] * n + [shape((2, KP, own), BF)],
            [idx, keys, values, *qg],
            scratch=[pltpu.VMEM((n * rows, own), BF)] * 2 + [pltpu.VMEM((KP, n * rows), BF)] * 2,
            name="attention",
        )
        query_grads = [parts_q]
        accs.append(acc)
    else:
        order, by_block, acc = [int(c) for c in str(o["order"])[1:]], {}, None
        for k in order:
            first, last = k == order[0], k == order[-1]
            by_block[k], acc = call(
                functools.partial(attention_body, heads, first, last),
                [shape((rows + (o["pad2"] if k == 2 and o["pad2"] else o["pad"]), own), BF), shape((2, KP, own), BF if last else F32)],
                [idx, keys, values, qg[k]] + ([] if first else [acc]),
                name="attention",
            )
        query_grads = [[by_block[k] for k in range(n)]]
        accs.append(acc)
    na = len(accs)
    grads = []
    for a, acc in enumerate(accs):
        if o["agp"] == "relay" or (o["agp"] == "mixed" and a == 0):
            g_parts = over_line(acc)
            inner = jnp.logical_or(i == 1, i == 2)
            grads.append([acc, g_parts[1], jnp.where(inner, g_parts[2][1], g_parts[3][0]), jnp.where(inner, g_parts[2][0], g_parts[3][1])])
        else:
            grads.append([acc] + [to_line(acc, k) for k in range(1, n)])

    if o["rs"] == "two":
        keep, send = call(
            functools.partial(weight_pairs_body, own, na),
            [shape((2, width // nd, 2 * own), F32)] * 2,
            [idx, whole, *accs],
            name="weight",
        )
        pair = keep + lax.ppermute(send, "dp", swap(nd, 1))
        weight_grad = pair[0] + lax.ppermute(pair[1], "dp", swap(nd, 2))
    else:
        weight = call(
            functools.partial(weight_body, own, na),
            [shape((width // nd, 2 * own), F32)] * nd,
            [idx, whole, *accs],
            [grads[-1][1]] if o["rs"] == "late" else [],
            name="weight",
        )
        keep = weight[0]
        weight = [weight[0]] + [lax.ppermute(weight[a], "dp", swap(nd, a)) for a in range(1, nd)]

    last = grads[-1]
    ret2 = to_line(query_grads[0][2], 2) if o["pad2"] else None
    jw = dict(
        g12=[keep, last[1], last[2]],
        g1=[keep, last[1]],
        g0=[keep, *grads[0][1:]],
        g0l=[keep, *grads[0][1:], last[1], last[2]],
        gall=[keep, *grads[0][1:], *last[1:]],
        keys=[keys],
        acc=[keep],
    )[o["jw"]] + ([ret2] if o["pad2"] else [])
    w_across = over_plane(w_line)
    w_own = call(
        join_body, [shape((n, n, w_rows, 2 * own), BF)], [idx, *w_across], jw, name="join_weights"
    )[0]
    w_core = over_cores(w_own)
    w_all = call(
        functools.partial(arrange_body, own),
        [shape((2, width, width), BF)],
        [idx, w_own, w_core],
        [keep, last[1]],
        name="arrange_weight",
    )[0]

    gate_on = dict(g2=[last[2]], g1=[last[1]], g3=[last[3]], none=[])[o["late"]]
    flat = [x for parts_q in query_grads for x in parts_q[1:]]
    late = gate(flat, gate_on, "hold_query_grads") if gate_on else flat
    returned = []
    for k in range(n):
        for a in range(na):
            if k == 2 and o["pad2"]:
                returned.append(ret2)
            else:
                returned.append(to_line(late[a * (n - 1) + k - 1], k) if k else query_grads[a][0])

    tail_in = [idx, *(grads[a][k] for k in range(n) for a in range(na)), w_all, length_proj.reshape(rows, 2 * KP), tokens]
    *terms, input_grad = call(
        functools.partial(tail_body, nd),
        [shape((rows // nd, 2 * KP), F32)] * nd + [shape((rows, width), BF)],
        tail_in,
        scratch=[pltpu.VMEM((2 * KP, width), BF), pltpu.VMEM((rows, 2 * KP), F32)],
        name="tail",
    )
    terms = [terms[0]] + [lax.ppermute(terms[a], "dp", swap(nd, a)) for a in range(1, nd)]
    query_grad = call(
        functools.partial(place_body, n, own),
        [shape((rows, width), BF)],
        [idx, *returned],
        [terms[0]],
        name="place",
    )[0]
    if o["sum"] == "pallas":
        length_grad = call(sum_body, [shape((rows // nd, 2, KP), F32)], [idx, *terms], [query_grad] if o["lq"] else [], name="sum_terms")[0]
    else:
        length_grad = (terms[0] + terms[1] + terms[2] + terms[3]).reshape(-1, 2, KP)

    if o["rs"] != "two":
        hold = dict(place=[query_grad], lt=[length_grad], none=[], t1=[terms[1]])[o["ws"]]
        weight_grad = call(sum_body, [shape((width // nd, 2, own), F32)], [idx, *weight], hold, name="sum_weight")[0]
    else:
        weight_grad = weight_grad.reshape(-1, 2, own)
    return query_grad[None], input_grad[None], length_grad, weight_grad


def by_positions(inputs, queries, cotangent, length_proj, key_value_weight):
    scale = DH ** (-0.5)
    tokens = inputs[0]
    query_row_block = queries[0]
    grad_rows = cotangent[0]
    rows = tokens.shape[0]
    full_width = key_value_weight.shape[0]
    compress = jnp.einsum("lsk,ld->skd", length_proj, tokens, preferred_element_type=jnp.float32)
    length_compressed = lax.psum(compress, "ctx").astype(jnp.bfloat16)
    own_proj = jnp.einsum(
        "skd,dsc->skc", length_compressed, key_value_weight, preferred_element_type=jnp.float32
    ).astype(jnp.bfloat16)
    length_projected = lax.all_gather(own_proj, "ctx", axis=2, tiled=True)
    keys = length_projected[0].reshape(KP, HEADS, DH)
    values = length_projected[1].reshape(KP, HEADS, DH)
    query_heads = query_row_block.reshape(rows, HEADS, DH)
    grad_heads = grad_rows.reshape(rows, HEADS, DH)
    scores = (
        jnp.einsum("lhd,khd->hlk", query_heads, keys, preferred_element_type=jnp.float32) * scale
    )
    probs = jax.nn.softmax(scores, axis=-1)
    probs_low = probs.astype(jnp.bfloat16)
    dprobs = jnp.einsum("lhd,khd->hlk", grad_heads, values, preferred_element_type=jnp.float32)
    delta = jnp.sum(probs * dprobs, axis=-1, keepdims=True)
    dscores = (probs * (dprobs - delta) * scale).astype(jnp.bfloat16)
    query_grad = jnp.einsum(
        "hlk,khd->lhd", dscores, keys, preferred_element_type=jnp.float32
    ).astype(jnp.bfloat16)
    query_grad = query_grad.reshape(1, rows, full_width)
    key_part = jnp.einsum("hlk,lhd->khd", dscores, query_heads, preferred_element_type=jnp.float32)
    value_part = jnp.einsum(
        "hlk,lhd->khd", probs_low, grad_heads, preferred_element_type=jnp.float32
    )
    partial_grad = jnp.stack([key_part.reshape(KP, full_width), value_part.reshape(KP, full_width)])
    own_grad = lax.psum_scatter(partial_grad, "ctx", scatter_dimension=2, tiled=True).astype(
        jnp.bfloat16
    )
    grad_term = jnp.einsum(
        "skc,dsc->skd", own_grad, key_value_weight, preferred_element_type=jnp.float32
    )
    compression_gradient = lax.psum(grad_term, "ctx").astype(jnp.bfloat16)
    input_grad = jnp.einsum(
        "lsk,skd->ld", length_proj, compression_gradient, preferred_element_type=jnp.float32
    ).astype(jnp.bfloat16)
    input_grad = input_grad.reshape(1, rows, full_width)
    length_grad = lax.psum_scatter(
        jnp.einsum("ld,skd->lsk", tokens, compression_gradient, preferred_element_type=jnp.float32),
        "dp",
        scatter_dimension=0,
        tiled=True,
    )
    weight_grad = lax.psum_scatter(
        jnp.einsum("skd,skc->dsc", length_compressed, own_grad, preferred_element_type=jnp.float32),
        "dp",
        scatter_dimension=0,
        tiled=True,
    )
    return (query_grad, input_grad, length_grad, weight_grad)


def solution(mesh):
    ng, n, nd = (mesh.shape[a] for a in ("groups", "ctx", "dp"))

    def local(*args):
        rows, width = args[0].shape[1:]
        fits = ng == 2 and n == 4 and nd == 4 and width % (n * 128) == 0 and HEADS % n == 0 and rows % 128 == 0
        if fits:
            return by_heads(ng, n, nd, *args)
        return by_positions(*args)

    in_specs = (
        P(("groups", "dp"), "ctx", None),
        P(("groups", "dp"), "ctx", None),
        P(("groups", "dp"), "ctx", None),
        P("ctx", None, None),
        P(None, None, "ctx"),
    )
    out_specs = (
        P(("groups", "dp"), "ctx", None),
        P(("groups", "dp"), "ctx", None),
        P(("groups", "ctx", "dp"), None, None),
        P(("groups", "dp"), None, "ctx"),
    )
    return jax.shard_map(local, mesh=mesh, in_specs=in_specs, out_specs=out_specs, check_vma=False)
```

```python
import functools

import jax
import jax.numpy as jnp
from jax import lax
from jax.experimental import pallas as pl
from jax.experimental.pallas import tpu as pltpu
from jax.sharding import PartitionSpec as P

HEADS = 16
DH = 64
KP = 256
BF = jnp.bfloat16
F32 = jnp.float32
VMEM_LIMIT = 24 * 1024 * 1024


def dot(a, b, ca, cb):
    return lax.dot_general(a, b, (((ca,), (cb,)), ((), ())), preferred_element_type=F32)


def call(body, outs, args, after=(), scratch=(), name=None):
    vmem = pl.BlockSpec(memory_space=pltpu.VMEM)

    def run(*refs):
        body(*refs[: len(args)], *refs[len(args) + len(after) :])

    return pl.pallas_call(
        run,
        out_shape=outs,
        in_specs=[pl.BlockSpec(memory_space=pltpu.SMEM)]
        + [vmem] * (len(args) - 1)
        + [pl.BlockSpec(memory_space=pl.ANY)] * len(after),
        out_specs=[vmem] * len(outs),
        scratch_shapes=list(scratch),
        compiler_params=pltpu.CompilerParams(vmem_limit_bytes=VMEM_LIMIT),
        cost_estimate=pl.CostEstimate(flops=1, bytes_accessed=1, transcendentals=0),
        name=name,
    )(*args, *after)


def shape(dims, dtype):
    return jax.ShapeDtypeStruct(dims, dtype)


def pack_body(n, own, idx, *rest):
    x, outs = rest[0], rest[1:]
    for k in range(n):
        col = pl.multiple_of((idx[0] ^ k) * own, own)
        outs[k][...] = x[:, pl.ds(col, own)]


def pack_pair_body(own, k, idx, q, g, out):
    col = pl.multiple_of((idx[0] ^ k) * own, own)
    out[0] = q[:, pl.ds(col, own)]
    out[1] = g[:, pl.ds(col, own)]


def join_body(idx, *rest):
    out = rest[-1]
    for k, x in enumerate(rest[:-1]):
        out[k] = x[...]


def slice_body(idx, x, out):
    rows = out.shape[0]
    out[...] = x[pl.ds(pl.multiple_of(idx[2] * rows, rows), rows), :]


def compress_body(n, plane, rows, idx, e_own, e_core, *rest):
    blocks, out, e_all = rest[:n], rest[n], rest[n + 1]
    part = rows // plane
    for c, e in enumerate((e_own, e_core)):
        for a in range(plane // 2):
            piece = idx[2 + a] ^ c
            for k in range(n):
                row = pl.multiple_of(k * rows + piece * part, 16)
                e_all[pl.ds(row, part), :] = e[a, k]
    total = dot(e_all[0:rows, :], blocks[0][...], 0, 0)
    for k in range(1, n):
        total += dot(e_all[k * rows : (k + 1) * rows, :], blocks[k][...], 0, 0)
    out[...] = total.astype(BF)


def pick(inner, near, far):
    return jnp.where(inner, near, far)


def project_body(own, idx, mine, side, near, far, w, keys, values, whole):
    inner = (idx[0] == 1) | (idx[0] == 2)
    whole[0] = mine[...]
    whole[1] = side[...]
    for a in range(2):
        whole[2 + a] = pick(inner, near[1 - a], far[a])
    for s, out in enumerate((keys, values)):
        total = None
        for k in range(4):
            row = pl.multiple_of((idx[0] ^ k) * own, own)
            term = dot(whole[k, s * KP : (s + 1) * KP, :], w[pl.ds(row, own), s * own : (s + 1) * own], 1, 0)
            total = term if total is None else total + term
        out[...] = total.astype(BF)


def attention_body(n, half, idx, keys, values, *rest):
    pairs, outs, (out, q_all, g_all, p_all, ds_all) = rest[:n], rest[n : 2 * n], rest[2 * n :]
    rows = pairs[0].shape[1]
    width = out.shape[2]
    cols = slice(half * width, (half + 1) * width)
    kk, vv = keys[:, cols], values[:, cols]
    for k in range(n):
        q_all[k * rows : (k + 1) * rows, :] = pairs[k][0, :, cols]
        g_all[k * rows : (k + 1) * rows, :] = pairs[k][1, :, cols]
    scale = DH**-0.5
    lane = lax.broadcasted_iota(jnp.int32, kk.shape, 1)
    grad_q = [None] * n
    key_part = value_part = None
    for h in range(width // DH):
        mask = (lane >= h * DH) & (lane < (h + 1) * DH)
        k_h = jnp.where(mask, kk, jnp.zeros_like(kk))
        v_h = jnp.where(mask, vv, jnp.zeros_like(vv))
        for k in range(n):
            block = slice(k * rows, (k + 1) * rows)
            scores = dot(k_h, q_all[block, :], 1, 1)
            e = jnp.exp((scores - jnp.max(scores, axis=0, keepdims=True)) * scale)
            p = e * (1.0 / jnp.sum(e, axis=0, keepdims=True))
            dp = dot(v_h, g_all[block, :], 1, 1)
            delta = jnp.sum(p * dp, axis=0, keepdims=True)
            ds = (p * (dp - delta) * scale).astype(BF)
            p_all[:, block] = p.astype(BF)
            ds_all[:, block] = ds
            term = dot(ds, k_h, 0, 0)
            grad_q[k] = term if h == 0 else grad_q[k] + term
        term_k = jnp.where(mask, dot(ds_all[...], q_all[...], 1, 0), 0.0)
        term_v = jnp.where(mask, dot(p_all[...], g_all[...], 1, 0), 0.0)
        key_part = term_k if h == 0 else key_part + term_k
        value_part = term_v if h == 0 else value_part + term_v
    for k in range(n):
        outs[k][...] = grad_q[k].astype(BF)
    out[0] = key_part.astype(BF)
    out[1] = value_part.astype(BF)


def weight_body(own, idx, whole, grad, *outs):
    for a, out in enumerate(outs):
        k = (idx[1] ^ a) ^ idx[0]
        for s in range(2):
            out[:, s * own : (s + 1) * own] = dot(whole[k, s * KP : (s + 1) * KP, :], grad[s], 0, 0)


def arrange_body(own, idx, w_own, w_core, out):
    part = w_own.shape[2]
    for c, w in enumerate((w_own, w_core)):
        for a in range(w.shape[0]):
            row = pl.multiple_of((idx[2 + a] ^ c) * part, part)
            for k in range(w.shape[1]):
                for s in range(2):
                    out[s, pl.ds(row, part), k * own : (k + 1) * own] = w[a, k, :, s * own : (s + 1) * own]


def tail_body(nd, idx, *rest):
    length_terms, (input_grad, cg, terms) = rest[-3 - nd : -3], rest[-3:]
    grads, (w, e, x) = rest[: -6 - nd], rest[-6 - nd : -3 - nd]
    for s in range(2):
        grad = jnp.concatenate([part[s] for part in grads], axis=1)
        cg[s * KP : (s + 1) * KP, :] = dot(grad, w[s], 1, 1).astype(BF)
    both = cg[...]
    terms[...] = dot(x[...], both, 1, 1)
    rows = x.shape[0] // nd
    for a in range(nd):
        length_terms[a][...] = terms[pl.ds(pl.multiple_of((idx[1] ^ a) * rows, 16), rows), :]
    input_grad[...] = dot(e[...], both, 1, 0).astype(BF)


def sum_body(idx, *rest):
    out = rest[-1]
    total = rest[0][...]
    for x in rest[1:-1]:
        total = total + x[...]
    for s in range(2):
        out[:, s, :] = total[:, s * KP : (s + 1) * KP]


def place_body(n, own, idx, *rest):
    out = rest[-1]
    parts = (len(rest) - 1) // n
    width = own // parts
    for k in range(n):
        col = pl.multiple_of((idx[0] ^ k) * own, own)
        for a in range(parts):
            out[:, pl.ds(col + a * width, width)] = rest[k * parts + a][: out.shape[0], :]


def by_heads(ng, n, nd, inputs, queries, cotangent, length_proj, key_value_weight):
    tokens, query_rows, grad_rows = inputs[0], queries[0], cotangent[0]
    rows, width = tokens.shape
    own = width // n
    plane = ng * nd
    g, i, d = lax.axis_index("groups"), lax.axis_index("ctx"), lax.axis_index("dp")
    m = g * nd + d
    flips = [(gy, dx) for gy in range(2) for dx in range(2)]
    idx = jnp.stack([i, d] + [(g ^ gy) * nd + (d ^ (2 * dx)) for gy, dx in flips]).astype(jnp.int32)

    def swap(axis_size, a):
        return [(j, j ^ a) for j in range(axis_size)]

    def to_line(x, k):
        return lax.ppermute(x, "ctx", swap(n, k))

    def over_line(x, after):
        side = to_line(x, 1)
        near = [lax.ppermute(x, "ctx", [(1, 2), (2, 1)]), lax.ppermute(x, "ctx", [(0, 2), (3, 1)])]
        near = call(join_body, [shape((2, *x.shape), BF)], [idx, *near], after, name="join_near")[0]
        far = lax.ppermute(near, "ctx", [(1, 0), (2, 3)])
        return x, side, near, far

    def over_plane(x):
        across = [x]
        for gy, dx in flips[1:]:
            perm = [
                (a * nd + b, (a ^ gy) * nd + (b ^ (2 * dx))) for a in range(ng) for b in range(nd)
            ]
            across.append(lax.ppermute(x, ("groups", "dp"), perm))
        return across

    def over_cores(x):
        return lax.ppermute(x, "dp", swap(nd, 1))

    def pack_queries(k, after):
        return call(
            functools.partial(pack_pair_body, own, k),
            [shape((2, rows, own), BF)],
            [idx, query_rows, grad_rows],
            after,
            name="pack_queries",
        )[0]

    part = rows // plane
    piece = lax.dynamic_slice_in_dim(length_proj, m * part, part, 0).reshape(part, 2 * KP)
    blocks = call(
        functools.partial(pack_body, n, own), [shape((rows, own), BF)] * n, [idx, tokens], name="pack_inputs"
    )
    pieces = [piece] + [to_line(piece, k) for k in range(1, n)]
    blocks = [blocks[0]] + [to_line(blocks[k], k) for k in range(1, n)]
    line = call(
        join_body, [shape((n, part, 2 * KP), BF)], [idx, *pieces], name="join_pieces"
    )[0]
    across = over_plane(line)
    packed = [pack_queries(k, [line]) for k in range(n)]
    e_own = call(
        join_body,
        [shape((n, n, part, 2 * KP), BF)],
        [idx, *across],
        [*blocks[2:], *packed],
        name="join_lines",
    )[0]
    e_core = over_cores(e_own)
    w = key_value_weight.reshape(width, 2 * own)
    w_rows = width // plane
    compressed = call(
        functools.partial(compress_body, n, plane, rows),
        [shape((2 * KP, own), BF)],
        [idx, e_own, e_core, *blocks],
        packed[1:],
        [pltpu.VMEM((n * rows, 2 * KP), BF)],
        name="compress",
    )[0]
    qg = [packed[0]] + [to_line(packed[k], k) for k in range(1, n)]
    parts = over_line(compressed, [qg[1]])

    w_piece = call(slice_body, [shape((w_rows, 2 * own), BF)], [idx, w], [parts[1]], name="slice_weight")[0]
    w_parts = [w_piece] + [to_line(w_piece, k) for k in range(1, n)]
    w_line = call(join_body, [shape((n, w_rows, 2 * own), BF)], [idx, *w_parts], name="join_weight")[0]
    keys, values, whole = call(
        functools.partial(project_body, own),
        [shape((KP, own), BF)] * 2 + [shape((n, 2 * KP, own), BF)],
        [idx, *parts, w],
        [qg[2], packed[1], w_line],
        name="project",
    )

    *query_grads, acc = call(
        functools.partial(attention_body, n, 0),
        [shape((rows, own), BF)] * n + [shape((2, KP, own), BF)],
        [idx, keys, values, *qg],
        scratch=[pltpu.VMEM((n * rows, own), BF)] * 2 + [pltpu.VMEM((KP, n * rows), BF)] * 2,
        name="attention",
    )
    grads = [acc] + [to_line(acc, k) for k in range(1, n)]

    weight = call(
        functools.partial(weight_body, own),
        [shape((width // nd, 2 * own), F32)] * nd,
        [idx, whole, acc],
        name="weight",
    )
    keep = weight[0]
    weight = [keep] + [lax.ppermute(weight[a], "dp", swap(nd, a)) for a in range(1, nd)]

    w_across = over_plane(w_line)
    w_own = call(
        join_body,
        [shape((n, n, w_rows, 2 * own), BF)],
        [idx, *w_across],
        [keep, grads[1], grads[2]],
        name="join_weights",
    )[0]
    w_core = over_cores(w_own)
    w_all = call(
        functools.partial(arrange_body, own),
        [shape((2, width, width), BF)],
        [idx, w_own, w_core],
        [keep, grads[1]],
        name="arrange_weight",
    )[0]

    returned = [query_grads[0]] + [to_line(query_grads[k], k) for k in range(1, n)]

    tail_in = [idx, *grads, w_all, length_proj.reshape(rows, 2 * KP), tokens]
    *terms, input_grad = call(
        functools.partial(tail_body, nd),
        [shape((rows // nd, 2 * KP), F32)] * nd + [shape((rows, width), BF)],
        tail_in,
        scratch=[pltpu.VMEM((2 * KP, width), BF), pltpu.VMEM((rows, 2 * KP), F32)],
        name="tail",
    )
    terms = [terms[0]] + [lax.ppermute(terms[a], "dp", swap(nd, a)) for a in range(1, nd)]
    query_grad = call(
        functools.partial(place_body, n, own),
        [shape((rows, width), BF)],
        [idx, *returned],
        [terms[0]],
        name="place",
    )[0]
    length_grad = call(sum_body, [shape((rows // nd, 2, KP), F32)], [idx, *terms], name="sum_terms")[0]
    weight_grad = call(sum_body, [shape((width // nd, 2, own), F32)], [idx, *weight], name="sum_weight")[0]
    return query_grad[None], input_grad[None], length_grad, weight_grad


def by_positions(inputs, queries, cotangent, length_proj, key_value_weight):
    scale = DH ** (-0.5)
    tokens = inputs[0]
    query_row_block = queries[0]
    grad_rows = cotangent[0]
    rows = tokens.shape[0]
    full_width = key_value_weight.shape[0]
    compress = jnp.einsum("lsk,ld->skd", length_proj, tokens, preferred_element_type=jnp.float32)
    length_compressed = lax.psum(compress, "ctx").astype(jnp.bfloat16)
    own_proj = jnp.einsum(
        "skd,dsc->skc", length_compressed, key_value_weight, preferred_element_type=jnp.float32
    ).astype(jnp.bfloat16)
    length_projected = lax.all_gather(own_proj, "ctx", axis=2, tiled=True)
    keys = length_projected[0].reshape(KP, HEADS, DH)
    values = length_projected[1].reshape(KP, HEADS, DH)
    query_heads = query_row_block.reshape(rows, HEADS, DH)
    grad_heads = grad_rows.reshape(rows, HEADS, DH)
    scores = (
        jnp.einsum("lhd,khd->hlk", query_heads, keys, preferred_element_type=jnp.float32) * scale
    )
    probs = jax.nn.softmax(scores, axis=-1)
    probs_low = probs.astype(jnp.bfloat16)
    dprobs = jnp.einsum("lhd,khd->hlk", grad_heads, values, preferred_element_type=jnp.float32)
    delta = jnp.sum(probs * dprobs, axis=-1, keepdims=True)
    dscores = (probs * (dprobs - delta) * scale).astype(jnp.bfloat16)
    query_grad = jnp.einsum(
        "hlk,khd->lhd", dscores, keys, preferred_element_type=jnp.float32
    ).astype(jnp.bfloat16)
    query_grad = query_grad.reshape(1, rows, full_width)
    key_part = jnp.einsum("hlk,lhd->khd", dscores, query_heads, preferred_element_type=jnp.float32)
    value_part = jnp.einsum(
        "hlk,lhd->khd", probs_low, grad_heads, preferred_element_type=jnp.float32
    )
    partial_grad = jnp.stack([key_part.reshape(KP, full_width), value_part.reshape(KP, full_width)])
    own_grad = lax.psum_scatter(partial_grad, "ctx", scatter_dimension=2, tiled=True).astype(
        jnp.bfloat16
    )
    grad_term = jnp.einsum(
        "skc,dsc->skd", own_grad, key_value_weight, preferred_element_type=jnp.float32
    )
    compression_gradient = lax.psum(grad_term, "ctx").astype(jnp.bfloat16)
    input_grad = jnp.einsum(
        "lsk,skd->ld", length_proj, compression_gradient, preferred_element_type=jnp.float32
    ).astype(jnp.bfloat16)
    input_grad = input_grad.reshape(1, rows, full_width)
    length_grad = lax.psum_scatter(
        jnp.einsum("ld,skd->lsk", tokens, compression_gradient, preferred_element_type=jnp.float32),
        "dp",
        scatter_dimension=0,
        tiled=True,
    )
    weight_grad = lax.psum_scatter(
        jnp.einsum("skd,skc->dsc", length_compressed, own_grad, preferred_element_type=jnp.float32),
        "dp",
        scatter_dimension=0,
        tiled=True,
    )
    return (query_grad, input_grad, length_grad, weight_grad)


def solution(mesh):
    ng, n, nd = (mesh.shape[a] for a in ("groups", "ctx", "dp"))

    def local(*args):
        rows, width = args[0].shape[1:]
        fits = ng == 2 and n == 4 and nd == 4 and width % (n * 128) == 0 and HEADS % n == 0 and rows % 128 == 0
        if fits:
            return by_heads(ng, n, nd, *args)
        return by_positions(*args)

    in_specs = (
        P(("groups", "dp"), "ctx", None),
        P(("groups", "dp"), "ctx", None),
        P(("groups", "dp"), "ctx", None),
        P("ctx", None, None),
        P(None, None, "ctx"),
    )
    out_specs = (
        P(("groups", "dp"), "ctx", None),
        P(("groups", "dp"), "ctx", None),
        P(("groups", "ctx", "dp"), None, None),
        P(("groups", "dp"), None, "ctx"),
    )
    return jax.shard_map(local, mesh=mesh, in_specs=in_specs, out_specs=out_specs, check_vma=False)
```

```python
import functools

import jax
import jax.numpy as jnp
from jax import lax
from jax.experimental import pallas as pl
from jax.experimental.pallas import tpu as pltpu
from jax.sharding import PartitionSpec as P

HEADS = 16
DH = 64
KP = 256
BF = jnp.bfloat16
F32 = jnp.float32
LOG2_E = 1.4426950408889634
VMEM_LIMIT = 24 * 1024 * 1024


def dot(a, b, ca, cb):
    return lax.dot_general(a, b, (((ca,), (cb,)), ((), ())), preferred_element_type=F32)


def call(body, outs, args, after=(), scratch=(), name=None):
    vmem = pl.BlockSpec(memory_space=pltpu.VMEM)

    def run(*refs):
        body(*refs[: len(args)], *refs[len(args) + len(after) :])

    return pl.pallas_call(
        run,
        out_shape=outs,
        in_specs=[pl.BlockSpec(memory_space=pltpu.SMEM)]
        + [vmem] * (len(args) - 1)
        + [pl.BlockSpec(memory_space=pl.ANY)] * len(after),
        out_specs=[vmem] * len(outs),
        scratch_shapes=list(scratch),
        compiler_params=pltpu.CompilerParams(vmem_limit_bytes=VMEM_LIMIT),
        cost_estimate=pl.CostEstimate(flops=1, bytes_accessed=1, transcendentals=0),
        name=name,
    )(*args, *after)


def shape(dims, dtype):
    return jax.ShapeDtypeStruct(dims, dtype)


def pack_body(n, own, idx, *rest):
    x, outs = rest[0], rest[1:]
    for k in range(n):
        col = pl.multiple_of((idx[0] ^ k) * own, own)
        outs[k][...] = x[:, pl.ds(col, own)]


def pack_pair_body(own, k, idx, q, g, out):
    col = pl.multiple_of((idx[0] ^ k) * own, own)
    out[0] = q[:, pl.ds(col, own)]
    out[1] = g[:, pl.ds(col, own)]


def join_body(idx, *rest):
    out = rest[-1]
    for k, x in enumerate(rest[:-1]):
        out[k] = x[...]


def slice_body(idx, x, out):
    rows = out.shape[0]
    out[...] = x[pl.ds(pl.multiple_of(idx[2] * rows, rows), rows), :]


def compress_body(n, plane, rows, idx, e_own, e_core, *rest):
    blocks, out, e_all = rest[:n], rest[n], rest[n + 1]
    part = rows // plane
    for c, e in enumerate((e_own, e_core)):
        for a in range(plane // 2):
            piece = idx[2 + a] ^ c
            for k in range(n):
                row = pl.multiple_of(k * rows + piece * part, 16)
                e_all[pl.ds(row, part), :] = e[a, k]
    total = dot(e_all[0:rows, :], blocks[0][...], 0, 0)
    for k in range(1, n):
        total += dot(e_all[k * rows : (k + 1) * rows, :], blocks[k][...], 0, 0)
    out[...] = total.astype(BF)


def pick(inner, near, far):
    return jnp.where(inner, near, far)


def project_body(own, idx, mine, side, near, far, w, keys, values, whole):
    inner = (idx[0] == 1) | (idx[0] == 2)
    whole[0] = mine[...]
    whole[1] = side[...]
    for a in range(2):
        whole[2 + a] = pick(inner, near[1 - a], far[a])
    for s, out in enumerate((keys, values)):
        total = None
        for k in range(4):
            row = pl.multiple_of((idx[0] ^ k) * own, own)
            term = dot(whole[k, s * KP : (s + 1) * KP, :], w[pl.ds(row, own), s * own : (s + 1) * own], 1, 0)
            total = term if total is None else total + term
        out[...] = total.astype(BF)


def attention_body(n, half, idx, keys, values, *rest):
    pairs, outs, (out, q_all, g_all, p_all, ds_all) = rest[:n], rest[n : 2 * n], rest[2 * n :]
    rows = pairs[0].shape[1]
    width = out.shape[2]
    cols = slice(half * width, (half + 1) * width)
    kk, vv = keys[:, cols], values[:, cols]
    for k in range(n):
        q_all[k * rows : (k + 1) * rows, :] = pairs[k][0, :, cols]
        g_all[k * rows : (k + 1) * rows, :] = pairs[k][1, :, cols]
    scale = DH**-0.5
    lane = lax.broadcasted_iota(jnp.int32, kk.shape, 1)
    grad_q = [None] * n
    key_part = value_part = None
    for h in range(width // DH):
        mask = (lane >= h * DH) & (lane < (h + 1) * DH)
        k_h = jnp.where(mask, kk, jnp.zeros_like(kk))
        v_h = jnp.where(mask, vv * scale, jnp.zeros_like(vv))
        for k in range(n):
            block = slice(k * rows, (k + 1) * rows)
            scores = dot(k_h, q_all[block, :], 1, 1)
            e = jnp.exp2((scores - jnp.max(scores, axis=0, keepdims=True)) * (scale * LOG2_E))
            p = e * (1.0 / jnp.sum(e, axis=0, keepdims=True))
            dp = dot(v_h, g_all[block, :], 1, 1)
            delta = jnp.sum(p * dp, axis=0, keepdims=True)
            ds = (p * (dp - delta)).astype(BF)
            p_all[:, block] = p.astype(BF)
            ds_all[:, block] = ds
            term = dot(ds, k_h, 0, 0)
            grad_q[k] = term if h == 0 else grad_q[k] + term
        term_k = jnp.where(mask, dot(ds_all[...], q_all[...], 1, 0), 0.0)
        term_v = jnp.where(mask, dot(p_all[...], g_all[...], 1, 0), 0.0)
        key_part = term_k if h == 0 else key_part + term_k
        value_part = term_v if h == 0 else value_part + term_v
    for k in range(n):
        outs[k][...] = grad_q[k].astype(BF)
    out[0] = key_part.astype(BF)
    out[1] = value_part.astype(BF)


def weight_body(own, idx, whole, grad, *outs):
    for a, out in enumerate(outs):
        k = (idx[1] ^ a) ^ idx[0]
        for s in range(2):
            out[:, s * own : (s + 1) * own] = dot(whole[k, s * KP : (s + 1) * KP, :], grad[s], 0, 0)


def arrange_body(own, idx, w_own, w_core, out):
    part = w_own.shape[2]
    for c, w in enumerate((w_own, w_core)):
        for a in range(w.shape[0]):
            row = pl.multiple_of((idx[2 + a] ^ c) * part, part)
            for k in range(w.shape[1]):
                for s in range(2):
                    out[s, pl.ds(row, part), k * own : (k + 1) * own] = w[a, k, :, s * own : (s + 1) * own]


def tail_body(nd, idx, *rest):
    length_terms, (input_grad, cg, terms) = rest[-3 - nd : -3], rest[-3:]
    grads, (w, e, x) = rest[: -6 - nd], rest[-6 - nd : -3 - nd]
    for s in range(2):
        grad = jnp.concatenate([part[s] for part in grads], axis=1)
        cg[s * KP : (s + 1) * KP, :] = dot(grad, w[s], 1, 1).astype(BF)
    both = cg[...]
    terms[...] = dot(x[...], both, 1, 1)
    rows = x.shape[0] // nd
    for a in range(nd):
        length_terms[a][...] = terms[pl.ds(pl.multiple_of((idx[1] ^ a) * rows, 16), rows), :]
    input_grad[...] = dot(e[...], both, 1, 0).astype(BF)


def sum_body(idx, *rest):
    out = rest[-1]
    total = rest[0][...]
    for x in rest[1:-1]:
        total = total + x[...]
    for s in range(2):
        out[:, s, :] = total[:, s * KP : (s + 1) * KP]


def place_body(n, own, idx, *rest):
    out = rest[-1]
    parts = (len(rest) - 1) // n
    width = own // parts
    for k in range(n):
        col = pl.multiple_of((idx[0] ^ k) * own, own)
        for a in range(parts):
            out[:, pl.ds(col + a * width, width)] = rest[k * parts + a][: out.shape[0], :]


def by_heads(ng, n, nd, inputs, queries, cotangent, length_proj, key_value_weight):
    tokens, query_rows, grad_rows = inputs[0], queries[0], cotangent[0]
    rows, width = tokens.shape
    own = width // n
    plane = ng * nd
    g, i, d = lax.axis_index("groups"), lax.axis_index("ctx"), lax.axis_index("dp")
    m = g * nd + d
    flips = [(gy, dx) for gy in range(2) for dx in range(2)]
    idx = jnp.stack([i, d] + [(g ^ gy) * nd + (d ^ (2 * dx)) for gy, dx in flips]).astype(jnp.int32)

    def swap(axis_size, a):
        return [(j, j ^ a) for j in range(axis_size)]

    def to_line(x, k):
        return lax.ppermute(x, "ctx", swap(n, k))

    def over_line(x, after):
        side = to_line(x, 1)
        near = [lax.ppermute(x, "ctx", [(1, 2), (2, 1)]), lax.ppermute(x, "ctx", [(0, 2), (3, 1)])]
        near = call(join_body, [shape((2, *x.shape), BF)], [idx, *near], after, name="join_near")[0]
        far = lax.ppermute(near, "ctx", [(1, 0), (2, 3)])
        return x, side, near, far

    def over_plane(x):
        across = [x]
        for gy, dx in flips[1:]:
            perm = [
                (a * nd + b, (a ^ gy) * nd + (b ^ (2 * dx))) for a in range(ng) for b in range(nd)
            ]
            across.append(lax.ppermute(x, ("groups", "dp"), perm))
        return across

    def over_cores(x):
        return lax.ppermute(x, "dp", swap(nd, 1))

    def pack_queries(k, after):
        return call(
            functools.partial(pack_pair_body, own, k),
            [shape((2, rows, own), BF)],
            [idx, query_rows, grad_rows],
            after,
            name="pack_queries",
        )[0]

    part = rows // plane
    piece = lax.dynamic_slice_in_dim(length_proj, m * part, part, 0).reshape(part, 2 * KP)
    blocks = call(
        functools.partial(pack_body, n, own), [shape((rows, own), BF)] * n, [idx, tokens], name="pack_inputs"
    )
    pieces = [piece] + [to_line(piece, k) for k in range(1, n)]
    blocks = [blocks[0]] + [to_line(blocks[k], k) for k in range(1, n)]
    line = call(
        join_body, [shape((n, part, 2 * KP), BF)], [idx, *pieces], name="join_pieces"
    )[0]
    across = over_plane(line)
    packed = [pack_queries(k, [line]) for k in range(n)]
    e_own = call(
        join_body,
        [shape((n, n, part, 2 * KP), BF)],
        [idx, *across],
        [*blocks[2:], *packed],
        name="join_lines",
    )[0]
    e_core = over_cores(e_own)
    w = key_value_weight.reshape(width, 2 * own)
    w_rows = width // plane
    compressed = call(
        functools.partial(compress_body, n, plane, rows),
        [shape((2 * KP, own), BF)],
        [idx, e_own, e_core, *blocks],
        packed[1:],
        [pltpu.VMEM((n * rows, 2 * KP), BF)],
        name="compress",
    )[0]
    qg = [packed[0]] + [to_line(packed[k], k) for k in range(1, n)]
    parts = over_line(compressed, [qg[1]])

    w_piece = call(slice_body, [shape((w_rows, 2 * own), BF)], [idx, w], [parts[1]], name="slice_weight")[0]
    w_parts = [w_piece] + [to_line(w_piece, k) for k in range(1, n)]
    w_line = call(join_body, [shape((n, w_rows, 2 * own), BF)], [idx, *w_parts], name="join_weight")[0]
    keys, values, whole = call(
        functools.partial(project_body, own),
        [shape((KP, own), BF)] * 2 + [shape((n, 2 * KP, own), BF)],
        [idx, *parts, w],
        [qg[2], packed[1], w_line],
        name="project",
    )

    *query_grads, acc = call(
        functools.partial(attention_body, n, 0),
        [shape((rows, own), BF)] * n + [shape((2, KP, own), BF)],
        [idx, keys, values, *qg],
        scratch=[pltpu.VMEM((n * rows, own), BF)] * 2 + [pltpu.VMEM((KP, n * rows), BF)] * 2,
        name="attention",
    )
    grads = [acc] + [to_line(acc, k) for k in range(1, n)]

    weight = call(
        functools.partial(weight_body, own),
        [shape((width // nd, 2 * own), F32)] * nd,
        [idx, whole, acc],
        name="weight",
    )
    keep = weight[0]
    weight = [keep] + [lax.ppermute(weight[a], "dp", swap(nd, a)) for a in range(1, nd)]

    w_across = over_plane(w_line)
    w_own = call(
        join_body,
        [shape((n, n, w_rows, 2 * own), BF)],
        [idx, *w_across],
        [keep, grads[1], grads[2]],
        name="join_weights",
    )[0]
    w_core = over_cores(w_own)
    w_all = call(
        functools.partial(arrange_body, own),
        [shape((2, width, width), BF)],
        [idx, w_own, w_core],
        [keep, grads[1]],
        name="arrange_weight",
    )[0]

    returned = [query_grads[0]] + [to_line(query_grads[k], k) for k in range(1, n)]

    tail_in = [idx, *grads, w_all, length_proj.reshape(rows, 2 * KP), tokens]
    *terms, input_grad = call(
        functools.partial(tail_body, nd),
        [shape((rows // nd, 2 * KP), F32)] * nd + [shape((rows, width), BF)],
        tail_in,
        scratch=[pltpu.VMEM((2 * KP, width), BF), pltpu.VMEM((rows, 2 * KP), F32)],
        name="tail",
    )
    terms = [terms[0]] + [lax.ppermute(terms[a], "dp", swap(nd, a)) for a in range(1, nd)]
    query_grad = call(
        functools.partial(place_body, n, own),
        [shape((rows, width), BF)],
        [idx, *returned],
        [terms[0]],
        name="place",
    )[0]
    length_grad = call(sum_body, [shape((rows // nd, 2, KP), F32)], [idx, *terms], name="sum_terms")[0]
    weight_grad = call(sum_body, [shape((width // nd, 2, own), F32)], [idx, *weight], name="sum_weight")[0]
    return query_grad[None], input_grad[None], length_grad, weight_grad


def by_positions(inputs, queries, cotangent, length_proj, key_value_weight):
    scale = DH ** (-0.5)
    tokens = inputs[0]
    query_row_block = queries[0]
    grad_rows = cotangent[0]
    rows = tokens.shape[0]
    full_width = key_value_weight.shape[0]
    compress = jnp.einsum("lsk,ld->skd", length_proj, tokens, preferred_element_type=jnp.float32)
    length_compressed = lax.psum(compress, "ctx").astype(jnp.bfloat16)
    own_proj = jnp.einsum(
        "skd,dsc->skc", length_compressed, key_value_weight, preferred_element_type=jnp.float32
    ).astype(jnp.bfloat16)
    length_projected = lax.all_gather(own_proj, "ctx", axis=2, tiled=True)
    keys = length_projected[0].reshape(KP, HEADS, DH)
    values = length_projected[1].reshape(KP, HEADS, DH)
    query_heads = query_row_block.reshape(rows, HEADS, DH)
    grad_heads = grad_rows.reshape(rows, HEADS, DH)
    scores = (
        jnp.einsum("lhd,khd->hlk", query_heads, keys, preferred_element_type=jnp.float32) * scale
    )
    probs = jax.nn.softmax(scores, axis=-1)
    probs_low = probs.astype(jnp.bfloat16)
    dprobs = jnp.einsum("lhd,khd->hlk", grad_heads, values, preferred_element_type=jnp.float32)
    delta = jnp.sum(probs * dprobs, axis=-1, keepdims=True)
    dscores = (probs * (dprobs - delta) * scale).astype(jnp.bfloat16)
    query_grad = jnp.einsum(
        "hlk,khd->lhd", dscores, keys, preferred_element_type=jnp.float32
    ).astype(jnp.bfloat16)
    query_grad = query_grad.reshape(1, rows, full_width)
    key_part = jnp.einsum("hlk,lhd->khd", dscores, query_heads, preferred_element_type=jnp.float32)
    value_part = jnp.einsum(
        "hlk,lhd->khd", probs_low, grad_heads, preferred_element_type=jnp.float32
    )
    partial_grad = jnp.stack([key_part.reshape(KP, full_width), value_part.reshape(KP, full_width)])
    own_grad = lax.psum_scatter(partial_grad, "ctx", scatter_dimension=2, tiled=True).astype(
        jnp.bfloat16
    )
    grad_term = jnp.einsum(
        "skc,dsc->skd", own_grad, key_value_weight, preferred_element_type=jnp.float32
    )
    compression_gradient = lax.psum(grad_term, "ctx").astype(jnp.bfloat16)
    input_grad = jnp.einsum(
        "lsk,skd->ld", length_proj, compression_gradient, preferred_element_type=jnp.float32
    ).astype(jnp.bfloat16)
    input_grad = input_grad.reshape(1, rows, full_width)
    length_grad = lax.psum_scatter(
        jnp.einsum("ld,skd->lsk", tokens, compression_gradient, preferred_element_type=jnp.float32),
        "dp",
        scatter_dimension=0,
        tiled=True,
    )
    weight_grad = lax.psum_scatter(
        jnp.einsum("skd,skc->dsc", length_compressed, own_grad, preferred_element_type=jnp.float32),
        "dp",
        scatter_dimension=0,
        tiled=True,
    )
    return (query_grad, input_grad, length_grad, weight_grad)


def solution(mesh):
    ng, n, nd = (mesh.shape[a] for a in ("groups", "ctx", "dp"))

    def local(*args):
        rows, width = args[0].shape[1:]
        fits = ng == 2 and n == 4 and nd == 4 and width % (n * 128) == 0 and HEADS % n == 0 and rows % 128 == 0
        if fits:
            return by_heads(ng, n, nd, *args)
        return by_positions(*args)

    in_specs = (
        P(("groups", "dp"), "ctx", None),
        P(("groups", "dp"), "ctx", None),
        P(("groups", "dp"), "ctx", None),
        P("ctx", None, None),
        P(None, None, "ctx"),
    )
    out_specs = (
        P(("groups", "dp"), "ctx", None),
        P(("groups", "dp"), "ctx", None),
        P(("groups", "ctx", "dp"), None, None),
        P(("groups", "dp"), None, "ctx"),
    )
    return jax.shard_map(local, mesh=mesh, in_specs=in_specs, out_specs=out_specs, check_vma=False)
```
